32 devices in a mesh: groups: 2 (over y), tile: 4 (over z), scan: 4 (over x, core).
Axes of the slice: x: 2, y: 2, z: 4, core: 2. Of those that a mesh axis runs over, the one named last changes fastest.
Arguments:
- object_field: float32 [2, 3072, 384], P(None, ('groups', 'tile')), parts along dimension 1, may hold values from -5 to 5
- probe_field: float32 [2, 512, 256], P(None, 'groups'), parts along dimension 1, may hold values from -6 to 6
- amplitudes: bfloat16 [8, 4, 4, 256, 256], P(('groups', 'tile'), 'scan'), parts along dimension 0, may hold values from 0.099609375 to 3
- anchors: int32 [8, 4, 4, 2], P(('groups', 'tile'), 'scan'), parts along dimension 0, may hold values from 8 to 376, as said below
- jitter: int32 [8, 4, 4, 2], P(('groups', 'tile'), 'scan'), parts along dimension 0, may hold values from -8 to 8
- counts: int32 [8, 4], P(('groups', 'tile'), 'scan'), parts along dimension 0, may hold values from 1 to 4, as said below
Outputs:
- object_out: float32 [2, 3072, 384], P(None, ('groups', 'tile')), parts along dimension 1
- probe_out: float32 [2, 512, 256], P(None, 'groups'), parts along dimension 1
The draws below stay inside these ranges and needn't reach their ends.
There are 2 independent parts, one for each index of `groups`. The reference program is written for one: setup_inputs(seed, part) draws one part's arguments, and reference() takes and returns one part's arrays. A program takes and returns all parts, laid end to end along the dimension named above; each array names one. Nothing has to cross between parts.
Inputs may be any that keep to these rules, and one draw needn't show every extreme that they name: `anchors`: with the jitter, a slot's row start lies in 0 to 384 within its tile, and its 256 rows stay within the tile and the next one; in the last tile they stay within the tile. Columns keep the window within the object. `counts`: slots at or after a device's count are not live; some device is full in every draw.
All inputs are finite; a program needn't handle non-finite values.
Results may differ from the reference program's by a relative error of at most 0.0063.
Values sent between devices are 32-bit elements; how exact they have to be, the bound alone decides.
A program may use at most 64 MiB of HBM per device.

```python
import math
import jax
import jax.numpy as jnp
from jax import lax

W = 256
TR = 384
OC = 384
S = 4
JIT = 8
ITERS = 2
NR = 1536
SCANS = 64
N_TILE = 4
N_SCAN = 4


def draw_anchors(key, part):
    key = jax.random.fold_in(key, 11)
    row_key, col_key = jax.random.split(key)
    upper_row = jnp.where(jnp.arange(N_TILE, dtype=jnp.int32) == N_TILE - 1, TR - W - JIT, TR - JIT)
    raw_bits = jax.random.randint(row_key, (N_TILE, N_SCAN, S), 0, 1 << 20)
    row_start = JIT + raw_bits % (upper_row[:, None, None] - JIT + 1)
    col_start = jax.random.randint(col_key, (N_TILE, N_SCAN, S), JIT, OC - W - JIT + 1)
    placed = jnp.stack([row_start, col_start], -1).astype(jnp.int32)
    placed = placed.at[0, 0, 0, 0].set(TR - JIT).at[0, 0, 0, 1].set(JIT)
    placed = placed.at[0, 0, 1, 0].set(JIT).at[0, 0, 1, 1].set(OC - W - JIT)
    return placed


def draw_counts(key, part):
    key = jax.random.fold_in(key, 23)
    value_key, spot_key = jax.random.split(key)
    values = jax.random.randint(value_key, (N_TILE * N_SCAN,), 1, S + 1)
    busy_spot = jax.random.randint(spot_key, (), 0, N_TILE * N_SCAN)
    values = values.at[busy_spot].set(S)
    return values.reshape(N_TILE, N_SCAN).astype(jnp.int32)


def set_ends(drawn, stream_key, smallest, top_value):
    extent = drawn.shape
    place = [jax.random.randint(jax.random.fold_in(stream_key, axis), (), 0, extent[axis]) for axis in range(len(extent))]
    drawn = drawn.at[tuple(place)].set(smallest)
    longest = extent.index(max(extent))
    place[longest] = (place[longest] + 1) % extent[longest]
    return drawn.at[tuple(place)].set(top_value)


def shard_levels(stream_key, dims, pieces, least, largest):
    factor_of, own = 1.0, jax.random.fold_in(stream_key, 6)
    for position, shards_of in pieces:
        draws = jnp.exp(jax.random.uniform(jax.random.fold_in(own, position), (shards_of,), jnp.float32, least / len(pieces), largest / len(pieces)))
        factor_of = factor_of * jnp.repeat(draws, dims[position] // shards_of).reshape([-1 if axis == position else 1 for axis in range(len(dims))])
    return factor_of


def bell_draw(key, extent, spread, limit, pieces=(), held_as=jnp.bfloat16):
    loudness = shard_levels(key, extent, pieces, -0.22, 0.18) if pieces else 1.0
    values = jax.random.normal(key, extent, jnp.float32) * spread * loudness
    return jnp.minimum(jnp.maximum(values, -limit), limit).astype(held_as)


def setup_inputs(seed: int = 0, part: int = 0) -> dict:
    keys = jax.random.split(jax.random.key(seed), 7)
    own_keys = jax.random.split(jax.random.fold_in(keys[6], part), 7)
    return {
        "object_field": bell_draw(own_keys[0], (2, NR, OC), 0.7, 5.0, ((1, 4),), jnp.float32),
        "probe_field": bell_draw(own_keys[1], (2, W, W), 1.0, 6.0, (), jnp.float32),
        "amplitudes": jnp.clip(jnp.exp(math.log(3.0) - 3.4051113 * jax.random.uniform(own_keys[2], (N_TILE, N_SCAN, S, W, W), jnp.float32) ** shard_levels(own_keys[2], (N_TILE, N_SCAN, S, W, W), ((0, 4), (1, 4)), -0.2, 0.2)), 0.099609375, 3.0).astype(jnp.bfloat16),
        "anchors": draw_anchors(jax.random.fold_in(jax.random.fold_in(keys[6], part), 71), part),
        "jitter": set_ends(jax.random.randint(own_keys[4], (N_TILE, N_SCAN, S, 2), 0 - JIT, JIT + 1), jax.random.fold_in(own_keys[4], 1), 0 - JIT, JIT).astype(jnp.int32),
        "counts": draw_counts(jax.random.fold_in(jax.random.fold_in(keys[6], part), 71), part),
    }


object_rate = 0.25

def tables(wave_size):
    indices = jnp.arange(wave_size, dtype=jnp.int32)
    angles = (indices[:, None] * indices[None, :] % wave_size).astype(jnp.float32) * (2.0 * math.pi / wave_size)
    cosine = jnp.cos(angles) / math.sqrt(wave_size)
    sines = jnp.sin(angles) / math.sqrt(wave_size)
    table_a = jnp.concatenate([jnp.concatenate([cosine, sines], 1), jnp.concatenate([-sines, cosine], 1)], 0)
    table_b = jnp.concatenate([jnp.concatenate([cosine, -sines], 1), jnp.concatenate([sines, cosine], 1)], 0)
    return (table_a.astype(jnp.bfloat16), table_b.astype(jnp.bfloat16))

def transform(waves, left_table, right_table):
    number, _, wave_size, _ = waves.shape
    stacked = waves.reshape(number, 2 * wave_size, wave_size)
    sectioned = jnp.einsum('ij,bjk->bik', left_table.astype(jnp.float32), stacked.astype(jnp.float32))
    sectioned = sectioned.astype(jnp.bfloat16).reshape(number, 2, wave_size, wave_size)
    sectioned = sectioned.transpose(0, 2, 1, 3).reshape(number, wave_size, 2 * wave_size)
    result = jnp.einsum('bij,jk->bik', sectioned.astype(jnp.float32), right_table.astype(jnp.float32))
    return result.reshape(number, wave_size, 2, wave_size).transpose(0, 2, 1, 3)

def scan_terms(patches, probe_field, measured, active, table_a, table_b):
    probe_re, probe_im = (probe_field[0], probe_field[1])
    patch_re, patch_im = (patches[:, 0], patches[:, 1])
    exit_wave = jnp.stack([probe_re * patch_re - probe_im * patch_im, probe_re * patch_im + probe_im * patch_re], 1).astype(jnp.bfloat16)
    spectrum = transform(exit_wave, table_a, table_b)
    power = spectrum[:, 0] ** 2 + spectrum[:, 1] ** 2
    factor = (measured.astype(jnp.float32) / jnp.sqrt(power + 0.25) - 1.0) * active[:, None, None]
    residual = (spectrum * factor[:, None]).astype(jnp.bfloat16)
    near_field = transform(residual, table_b, table_a)
    near_re, near_im = (near_field[:, 0], near_field[:, 1])
    object_step = jnp.stack([probe_re * near_re + probe_im * near_im, probe_re * near_im - probe_im * near_re], 1)
    probe_step = jnp.stack([lax.optimization_barrier(jnp.sum(patch_re * near_re + patch_im * near_im, 0)), lax.optimization_barrier(jnp.sum(patch_re * near_im - patch_im * near_re, 0))], 0)
    return (object_step, probe_step)

def reference(object_field, probe_field, amplitudes, anchors, jitter, counts):
    table_a, table_b = tables(W)
    root = jnp.zeros((), jnp.int32)
    starts = (anchors + jitter).reshape(N_TILE * N_SCAN, S, 2)
    row_base = jnp.repeat(jnp.arange(N_TILE, dtype=jnp.int32) * TR, N_SCAN)
    active = (jnp.arange(S, dtype=jnp.int32)[None, :] < counts.reshape(-1)[:, None]).astype(jnp.float32)
    measured = amplitudes.reshape(N_TILE * N_SCAN, S, W, W)
    for iteration in range(ITERS):
        padded = jnp.concatenate([object_field, jnp.zeros((2, W, OC), jnp.float32)], 1)

        def scan_block(totals, block_data):
            gradient, probe_total = totals
            base_row, start_pair, measured_block, active_block = block_data
            row_start = base_row + start_pair[:, 0]
            col_start = start_pair[:, 1]

            def window(row_one, col_one):
                return lax.dynamic_slice(padded, (root, row_one, col_one), (2, W, W))
            patches = jax.vmap(window)(row_start, col_start)
            object_step, probe_step = scan_terms(patches, probe_field, measured_block, active_block, table_a, table_b)

            def add_slot(slot, accum):
                current = lax.dynamic_slice(accum, (root, row_start[slot], col_start[slot]), (2, W, W))
                return lax.dynamic_update_slice(accum, current + object_step[slot], (root, row_start[slot], col_start[slot]))
            gradient = lax.fori_loop(0, S, add_slot, gradient)
            return ((gradient, probe_total + probe_step), None)
        zeros_grid = jnp.zeros(padded.shape, jnp.float32)
        zeros_probe = jnp.zeros(probe_field.shape, jnp.float32)
        (gradient, probe_total), _ = lax.scan(scan_block, (zeros_grid, zeros_probe), (row_base, starts, measured, active))
        strength = jnp.max(probe_field[0] ** 2 + probe_field[1] ** 2) + 1e-06
        object_field = object_field + object_rate * gradient[:, :NR] / strength
        probe_field = probe_field + probe_total / math.sqrt(SCANS)
    return (object_field, probe_field)
```

```python
import functools
import math

import jax
import jax.numpy as jnp
import numpy as np
from jax import lax
from jax.experimental import pallas as pl
from jax.experimental.pallas import tpu as pltpu
from jax.sharding import PartitionSpec as P

ITERS = 2
RATE = 0.25
CORES = 2
LANES = 128
CHUNK = 32


def tables(wave):
    index = np.arange(wave)
    angles = (index[:, None] * index[None, :] % wave) * (2.0 * math.pi / wave)
    cosine = np.cos(angles) / math.sqrt(wave)
    sines = np.sin(angles) / math.sqrt(wave)
    table_a = np.block([[cosine, sines], [-sines, cosine]])
    table_b = np.block([[cosine, -sines], [sines, cosine]])
    return (jnp.asarray(table_a, jnp.bfloat16), jnp.asarray(table_b, jnp.bfloat16))


def scan_kernel(
    starts, counts, padded, probe, amps, table_a, table_b, grad, probe_grad,
    window, terms, patch, waves, sections, field,
):
    slots, wave, _ = amps.shape
    columns = padded.shape[2]
    pieces = columns // LANES
    wide = wave // LANES
    lane = lax.broadcasted_iota(jnp.int32, (CHUNK, LANES), 1)

    for part in range(2):
        for p in range(pieces):
            window[part, p] = padded[part, :, p * LANES : (p + 1) * LANES]
    terms[...] = jnp.zeros(terms.shape, jnp.float32)
    probe_grad[...] = jnp.zeros(probe_grad.shape, jnp.float32)

    def dot(left, right):
        return jnp.dot(left, right, preferred_element_type=jnp.float32)

    def slot_step(slot, carry):
        row = starts[slot, 0]
        col = starts[slot, 1]
        live = jnp.where(slot < counts[0], 1.0, 0.0).astype(jnp.float32)
        back = lax.rem(LANES - lax.rem(col, LANES), LANES)
        ahead = lax.rem(col, LANES)
        skip = lax.div(col, LANES)
        low = lane < LANES - ahead
        high = lane >= ahead

        for top in range(0, wave, CHUNK):
            halves = []
            for part in range(2):
                turned = [
                    pltpu.roll(
                        window[part, p, pl.ds(row + top, CHUNK), :], back, 1
                    )
                    for p in range(pieces)
                ]
                turned.append(turned[-1])
                lanes_out = []
                for w in range(wide):
                    best = None
                    for k in range(pieces - wide + 1):
                        this = jnp.where(low, turned[w + k], turned[w + k + 1])
                        best = this if best is None else jnp.where(skip == k, this, best)
                    lanes_out.append(best)
                halves.append(jnp.concatenate(lanes_out, 1))
            real, imag = halves
            patch[0, top : top + CHUNK, :] = real
            patch[1, top : top + CHUNK, :] = imag
            p_re = probe[0, top : top + CHUNK, :]
            p_im = probe[1, top : top + CHUNK, :]
            waves[top : top + CHUNK, :] = (p_re * real - p_im * imag).astype(jnp.bfloat16)
            waves[wave + top : wave + top + CHUNK, :] = (p_re * imag + p_im * real).astype(
                jnp.bfloat16
            )

        sectioned = dot(table_a[...], waves[...]).astype(jnp.bfloat16)
        sections[:, :wave] = sectioned[:wave]
        sections[:, wave:] = sectioned[wave:]
        field[...] = dot(sections[...], table_b[...])

        for top in range(0, wave, CHUNK):
            real = field[top : top + CHUNK, :wave]
            imag = field[top : top + CHUNK, wave:]
            power = real * real + imag * imag
            measured = amps[slot, top : top + CHUNK, :].astype(jnp.float32)
            factor = (measured * lax.rsqrt(power + 0.25) - 1.0) * live
            waves[top : top + CHUNK, :] = (real * factor).astype(jnp.bfloat16)
            waves[wave + top : wave + top + CHUNK, :] = (imag * factor).astype(jnp.bfloat16)

        sectioned = dot(table_b[...], waves[...]).astype(jnp.bfloat16)
        sections[:, :wave] = sectioned[:wave]
        sections[:, wave:] = sectioned[wave:]
        field[...] = dot(sections[...], table_a[...])

        for top in range(0, wave, CHUNK):
            real = field[top : top + CHUNK, :wave]
            imag = field[top : top + CHUNK, wave:]
            p_re = probe[0, top : top + CHUNK, :]
            p_im = probe[1, top : top + CHUNK, :]
            w_re = patch[0, top : top + CHUNK, :]
            w_im = patch[1, top : top + CHUNK, :]
            probe_grad[0, top : top + CHUNK, :] += w_re * real + w_im * imag
            probe_grad[1, top : top + CHUNK, :] += w_re * imag - w_im * real
            steps = (p_re * real + p_im * imag, p_re * imag - p_im * real)
            for part in range(2):
                turned = [
                    pltpu.roll(steps[part][:, w * LANES : (w + 1) * LANES], ahead, 1)
                    for w in range(wide)
                ]
                zero = jnp.zeros((CHUNK, LANES), jnp.float32)

                def block(index):
                    return turned[index] if 0 <= index < wide else zero

                for p in range(pieces):
                    best = None
                    for k in range(pieces - wide + 1):
                        this = jnp.where(high, block(p - k), block(p - k - 1))
                        best = this if best is None else jnp.where(skip == k, this, best)
                    terms[part, p, pl.ds(row + top, CHUNK), :] += best
        return carry

    lax.fori_loop(0, slots, slot_step, 0)
    for part in range(2):
        for p in range(pieces):
            grad[part, :, p * LANES : (p + 1) * LANES] = terms[part, p]


def scan_terms(starts, counts, padded, probe, amps, table_a, table_b):
    slots, wave, _ = amps.shape
    _, extent, columns = padded.shape
    blocks = pltpu.VMEM((2, columns // LANES, extent, LANES), jnp.float32)
    vmem = pl.BlockSpec(memory_space=pltpu.VMEM)
    smem = pl.BlockSpec(memory_space=pltpu.SMEM)
    return pl.pallas_call(
        scan_kernel,
        out_shape=(
            jax.ShapeDtypeStruct(padded.shape, jnp.float32),
            jax.ShapeDtypeStruct(probe.shape, jnp.float32),
        ),
        in_specs=[smem, smem, vmem, vmem, vmem, vmem, vmem],
        out_specs=(vmem, vmem),
        scratch_shapes=[
            blocks,
            blocks,
            pltpu.VMEM((2, wave, wave), jnp.float32),
            pltpu.VMEM((2 * wave, wave), jnp.bfloat16),
            pltpu.VMEM((wave, 2 * wave), jnp.bfloat16),
            pltpu.VMEM((wave, 2 * wave), jnp.float32),
        ],
        compiler_params=pltpu.CompilerParams(vmem_limit_bytes=32 * 1024 * 1024),
        name="scan_terms",
    )(starts, counts, padded, probe, amps, table_a, table_b)


class Links:
    def __init__(self, send, recv, n_tile, n_scan):
        self.send, self.recv = send, recv
        self.used = 0
        self.drain = []
        self.n_tile = n_tile
        self.chips = n_scan // CORES
        self.tile = lax.axis_index("tile")
        self.scan = lax.axis_index("scan")
        self.chip = self.scan // CORES
        self.core = self.scan % CORES

    def other_core(self):
        return {"scan": self.chip * CORES + 1 - self.core}

    def chip_at(self, step):
        return (self.chip + step) % self.chips

    def on_chip(self, step):
        return {"scan": self.chip_at(step) * CORES + self.core}

    def greet(self, tiles):
        barrier = pltpu.get_barrier_semaphore()
        peers = [self.other_core()] + [self.on_chip(k) for k in range(1, self.chips)]
        peers += [{"tile": (self.tile + k) % self.n_tile} for k in tiles]
        for peer in peers:
            pl.semaphore_signal(
                barrier, inc=1, device_id=peer, device_id_type=pl.DeviceIdType.MESH
            )
        pl.semaphore_wait(barrier, len(peers))

    def copy(self, source, target, device, when=None):
        made = pltpu.make_async_remote_copy(
            src_ref=source,
            dst_ref=target,
            send_sem=self.send.at[self.used],
            recv_sem=self.recv.at[self.used],
            device_id=device,
            device_id_type=pl.DeviceIdType.MESH,
        )
        self.used += 1
        if when is None:
            made.start()
        else:
            pl.when(when)(made.start)
        self.drain.append((made, when))
        return made

    def finish(self):
        for made, when in self.drain:
            if when is None:
                made.wait_send()
            else:
                pl.when(when)(made.wait_send)


def on(when, action):
    if when is None:
        action()
    else:
        pl.when(when)(action)


def rim_kernel(n_tile, n_scan, wave, parts, own, padded, send, recv):
    links = Links(send, recv, n_tile, n_scan)
    rows = own.shape[1]
    chips, tile, core, chip = links.chips, links.tile, links.core, links.chip
    share = wave // chips
    some = share // parts
    above, below = tile > 0, tile < n_tile - 1
    tiles = sorted({1, n_tile - 1})
    links.greet(tiles)

    def at(owner, part, base):
        return pl.ds(base + owner * share + part * some, some)

    up = {"tile": (tile + n_tile - 1) % n_tile}
    first = [
        links.copy(own.at[core, at(chip, p, 0)], padded.at[core, at(chip, p, rows)], up, above)
        for p in range(parts)
    ]
    padded[:, :rows, :] = own[...]

    @pl.when(tile == n_tile - 1)
    def _():
        padded[:, rows:, :] = jnp.zeros((2, wave, own.shape[2]), jnp.float32)

    across, landed = [], []
    for p in range(parts):
        on(below, first[p].wait_recv)
        here = padded.at[core, at(chip, p, rows)]
        for k in range(1, chips):
            across.append((k, p, links.copy(here, here, links.on_chip(k), below)))
        landed.append(links.copy(here, here, links.other_core(), below))
    for k, p, made in across:
        on(below, made.wait_recv)
        here = padded.at[core, at(links.chip_at(chips - k), p, rows)]
        landed.append(links.copy(here, here, links.other_core(), below))
    for made in landed:
        on(below, made.wait_recv)
    links.finish()


def merge_kernel(
    n_tile, n_scan, scale, last, grad, probe_grad, old, probe, out, probe_out,
    core_in, core_probe, total, probe_total, rim_in, head_in, tail_in, probe_in,
    rim_sum, rim_back, probe_parts, send, recv,
):
    links = Links(send, recv, n_tile, n_scan)
    chips, tile, core, chip = links.chips, links.tile, links.core, links.chip
    wave = probe.shape[1]
    rows = grad.shape[1] - wave
    rest = rows - wave
    head, tail = wave // chips, rest // chips
    owners = probe_parts_of(n_tile, chips, wave)
    fine = head // owners
    above, below = tile > 0, tile < n_tile - 1
    down = {"tile": (tile + 1) % n_tile}
    up = {"tile": (tile + n_tile - 1) % n_tile}
    links.greet(range(1, n_tile))
    other = 1 - core
    partner = links.other_core()

    def to_core(first, count):
        span = pl.ds(first, count)
        return links.copy(grad.at[other, span], core_in.at[span], partner)

    got_rim = to_core(rows, wave)
    got_probe = links.copy(probe_grad.at[other], core_probe, partner)
    got_head = to_core(0, wave)
    got_tail = to_core(wave, rest)

    def fold(got, first, count, share, landing):
        got.wait_recv()
        span = pl.ds(first, count)
        total[span, :] = grad[core, span, :] + core_in[span, :]
        sent = []
        for k in range(1, chips):
            piece = total.at[pl.ds(first + links.chip_at(k) * share, share)]
            sent.append(links.copy(piece, landing.at[chip], links.on_chip(k)))
        return sent

    def gathered(sent, mine, landing):
        for made in sent:
            made.wait_recv()
        for k in range(1, chips):
            mine = mine + landing[links.chip_at(k)]
        return mine

    rim_sent = fold(got_rim, rows, wave, head, rim_in)
    got_probe.wait_recv()
    probe_total[...] = probe_grad[core] + core_probe[...]
    probe_sent = []
    for k in range(1, chips):
        piece = probe_total.at[pl.ds(links.chip_at(k) * head, head)]
        probe_sent.append(links.copy(piece, probe_in.at[chip], links.on_chip(k)))
    head_sent = fold(got_head, 0, wave, head, head_in)
    tail_sent = fold(got_tail, wave, rest, tail, tail_in)

    inverse = RATE / (
        jnp.max(probe[0] * probe[0] + probe[1] * probe[1], axis=(0, 1), keepdims=True) + 1e-06
    )

    rim_sum[...] = gathered(rim_sent, total[pl.ds(rows + chip * head, head), :], rim_in)
    rim_sent = links.copy(rim_sum, rim_back, down, below)

    mine = gathered(probe_sent, probe_total[pl.ds(chip * head, head), :], probe_in)
    probe_total[pl.ds(chip * head, head), :] = mine

    def owns(index):
        return None if owners == n_tile else index < owners

    spread = []
    for k in range(1, n_tile):
        to = (tile + k) % n_tile
        piece = jnp.minimum(to, owners - 1) if owners < n_tile else to
        spread.append(
            links.copy(
                probe_total.at[pl.ds(chip * head + piece * fine, fine)],
                probe_parts.at[tile],
                {"tile": to},
                owns(to),
            )
        )

    own_part = jnp.minimum(tile, owners - 1) if owners < n_tile else tile
    own_rows = pl.ds(chip * head + own_part * fine, fine)
    for made in spread:
        on(owns(tile), made.wait_recv)

    def close():
        sum_here = probe_total[own_rows, :]
        for k in range(1, n_tile):
            sum_here = sum_here + probe_parts[(tile + k) % n_tile]
        probe_out[core, own_rows, :] = probe[core, own_rows, :] + sum_here * scale

    on(owns(tile), close)
    place = probe_out.at[core, own_rows]
    probe_back = [
        links.copy(place, place, {"tile": (tile + k) % n_tile}, owns(tile))
        for k in range(1, n_tile)
    ]

    head_rows = pl.ds(chip * head, head)
    head_sum = gathered(head_sent, total[head_rows, :], head_in)
    on(above, rim_sent.wait_recv)
    back = jnp.where(above, rim_back[...], 0.0)
    out[core, head_rows, :] = old[core, head_rows, :] + inverse * (head_sum + back)
    here = out.at[core, head_rows]
    head_across = [links.copy(here, here, links.on_chip(k)) for k in range(1, chips)]
    rims = []
    if not last:
        rims.append(links.copy(here, out.at[core, pl.ds(rows + chip * head, head)], up, above))
    core_last = [(links.copy(here, here, partner), None)]

    tail_rows = pl.ds(wave + chip * tail, tail)
    tail_sum = gathered(tail_sent, total[tail_rows, :], tail_in)
    out[core, tail_rows, :] = old[core, tail_rows, :] + inverse * tail_sum
    here = out.at[core, tail_rows]
    tail_across = [links.copy(here, here, links.on_chip(k)) for k in range(1, chips)]
    core_last.append((links.copy(here, here, partner), None))

    for k, made in zip(range(1, n_tile), probe_back):
        on(owns((tile + n_tile - k) % n_tile), made.wait_recv)
    here = probe_out.at[core, pl.ds(chip * head, head)]
    probe_across = [links.copy(here, here, links.on_chip(k)) for k in range(1, chips)]
    core_last.append((links.copy(here, here, partner), None))

    for k in range(1, chips):
        head_across[k - 1].wait_recv()
        begin = links.chip_at(chips - k) * head
        here = out.at[core, pl.ds(begin, head)]
        if not last:
            rims.append(links.copy(here, out.at[core, pl.ds(rows + begin, head)], up, above))
        core_last.append((links.copy(here, here, partner), None))
    for k in range(1, chips):
        tail_across[k - 1].wait_recv()
        here = out.at[core, pl.ds(wave + links.chip_at(chips - k) * tail, tail)]
        core_last.append((links.copy(here, here, partner), None))
    for k in range(1, chips):
        probe_across[k - 1].wait_recv()
        here = probe_out.at[core, pl.ds(links.chip_at(chips - k) * head, head)]
        core_last.append((links.copy(here, here, partner), None))
    if not last:

        @pl.when(tile == n_tile - 1)
        def _():
            out[:, rows:, :] = jnp.zeros((2, wave, out.shape[2]), jnp.float32)

        for k, made in enumerate(rims):
            on(below, made.wait_recv)
            begin = links.chip_at((chips - k) % chips) * head
            here = out.at[core, pl.ds(rows + begin, head)]
            core_last.append((links.copy(here, here, partner, below), below))
    for made, when in core_last:
        on(when, made.wait_recv)
    links.finish()


def probe_parts_of(n_tile, chips, wave):
    owners = n_tile
    while (wave // chips) % owners or (wave // chips // owners) % 8:
        owners -= 1
    return owners


def first_rim(own, wave):
    n_tile, n_scan = lax.axis_size("tile"), lax.axis_size("scan")
    _, rows, columns = own.shape
    vmem = pl.BlockSpec(memory_space=pltpu.VMEM)
    parts = 2
    copies = parts * (2 * (n_scan // CORES) + 1)
    return pl.pallas_call(
        functools.partial(rim_kernel, n_tile, n_scan, wave, parts),
        out_shape=jax.ShapeDtypeStruct((2, rows + wave, columns), jnp.float32),
        in_specs=[vmem],
        out_specs=vmem,
        scratch_shapes=[pltpu.SemaphoreType.DMA((copies,)), pltpu.SemaphoreType.DMA((copies,))],
        compiler_params=pltpu.CompilerParams(
            collective_id=0, has_side_effects=True, vmem_limit_bytes=24 * 1024 * 1024
        ),
        name="first_rim",
    )(own)


def merge(grad, probe_grad, old, probe, scale, last, number):
    n_tile, n_scan = lax.axis_size("tile"), lax.axis_size("scan")
    chips = n_scan // CORES
    _, wave, _ = probe.shape
    _, extent, columns = grad.shape
    rows = extent - wave
    head, tail = wave // chips, (rows - wave) // chips
    fine = head // probe_parts_of(n_tile, chips, wave)
    vmem = pl.BlockSpec(memory_space=pltpu.VMEM)
    copies = 16 + 10 * chips + 2 * n_tile
    return pl.pallas_call(
        functools.partial(merge_kernel, n_tile, n_scan, scale, last),
        out_shape=(
            jax.ShapeDtypeStruct((2, rows if last else extent, columns), jnp.float32),
            jax.ShapeDtypeStruct(probe.shape, jnp.float32),
        ),
        in_specs=[vmem] * 4,
        out_specs=(vmem, vmem),
        scratch_shapes=[
            pltpu.VMEM((extent, columns), jnp.float32),
            pltpu.VMEM((wave, wave), jnp.float32),
            pltpu.VMEM((extent, columns), jnp.float32),
            pltpu.VMEM((wave, wave), jnp.float32),
            pltpu.VMEM((chips, head, columns), jnp.float32),
            pltpu.VMEM((chips, head, columns), jnp.float32),
            pltpu.VMEM((chips, tail, columns), jnp.float32),
            pltpu.VMEM((chips, head, wave), jnp.float32),
            pltpu.VMEM((head, columns), jnp.float32),
            pltpu.VMEM((head, columns), jnp.float32),
            pltpu.VMEM((n_tile, fine, wave), jnp.float32),
            pltpu.SemaphoreType.DMA((copies,)),
            pltpu.SemaphoreType.DMA((copies,)),
        ],
        compiler_params=pltpu.CompilerParams(
            collective_id=number, has_side_effects=True, vmem_limit_bytes=32 * 1024 * 1024
        ),
        name="merge_last" if last else "merge",
    )(grad, probe_grad, old, probe)


def body(object_field, probe_field, amplitudes, anchors, jitter, counts):
    wave = probe_field.shape[1]
    slots = amplitudes.shape[2]
    table_a, table_b = tables(wave)
    starts = (anchors + jitter)[0, 0]
    measured = amplitudes[0, 0]
    total_scans = slots * lax.axis_size("tile") * lax.axis_size("scan")
    scale = 1.0 / math.sqrt(total_scans)
    padded = first_rim(object_field, wave)
    probe = probe_field
    for iteration in range(ITERS):
        last = iteration == ITERS - 1
        grad, probe_grad = scan_terms(
            starts, counts[0], padded, probe, measured, table_a, table_b
        )
        padded, probe = merge(grad, probe_grad, padded, probe, scale, last, 1 + iteration)
    return (padded, probe)


def solution(mesh):
    in_specs = (
        P(None, ("groups", "tile"), None),
        P(None, "groups", None),
        P(("groups", "tile"), "scan", None, None, None),
        P(("groups", "tile"), "scan", None, None),
        P(("groups", "tile"), "scan", None, None),
        P(("groups", "tile"), "scan"),
    )
    out_specs = (P(None, ("groups", "tile"), None), P(None, "groups", None))
    return jax.shard_map(body, mesh=mesh, in_specs=in_specs, out_specs=out_specs, check_vma=False)
```

```python
import functools
import math

import jax
import jax.numpy as jnp
import numpy as np
from jax import lax
from jax.experimental import pallas as pl
from jax.experimental.pallas import tpu as pltpu
from jax.sharding import PartitionSpec as P

ITERS = 2
RATE = 0.25
CORES = 2
LANES = 128
CHUNK = 32


def tables(wave):
    index = np.arange(wave)
    angles = (index[:, None] * index[None, :] % wave) * (2.0 * math.pi / wave)
    cosine = np.cos(angles) / math.sqrt(wave)
    sines = np.sin(angles) / math.sqrt(wave)
    table_a = np.block([[cosine, sines], [-sines, cosine]])
    table_b = np.block([[cosine, -sines], [sines, cosine]])
    return (jnp.asarray(table_a, jnp.bfloat16), jnp.asarray(table_b, jnp.bfloat16))


def scan_kernel(
    anchors, jitter, counts, padded, probe, amps, table_a, table_b, grad, probe_grad,
    window, terms, patch, waves, sections, field,
):
    slots, wave = amps.shape[2:4]
    columns = padded.shape[2]
    pieces = columns // LANES
    wide = wave // LANES
    lane = lax.broadcasted_iota(jnp.int32, (CHUNK, LANES), 1)

    for part in range(2):
        for p in range(pieces):
            window[part, p] = padded[part, :, p * LANES : (p + 1) * LANES]
    terms[...] = jnp.zeros(terms.shape, jnp.float32)
    probe_grad[...] = jnp.zeros(probe_grad.shape, jnp.float32)

    def dot(left, right):
        return jnp.dot(left, right, preferred_element_type=jnp.float32)

    def slot_step(slot, carry):
        row = anchors[0, 0, slot, 0] + jitter[0, 0, slot, 0]
        col = anchors[0, 0, slot, 1] + jitter[0, 0, slot, 1]
        live = jnp.where(slot < counts[0, 0], 1.0, 0.0).astype(jnp.float32)
        back = lax.rem(LANES - lax.rem(col, LANES), LANES)
        ahead = lax.rem(col, LANES)
        skip = lax.div(col, LANES)
        low = lane < LANES - ahead
        high = lane >= ahead

        for top in range(0, wave, CHUNK):
            halves = []
            for part in range(2):
                turned = [
                    pltpu.roll(
                        window[part, p, pl.ds(row + top, CHUNK), :], back, 1
                    )
                    for p in range(pieces)
                ]
                turned.append(turned[-1])
                lanes_out = []
                for w in range(wide):
                    best = None
                    for k in range(pieces - wide + 1):
                        this = jnp.where(low, turned[w + k], turned[w + k + 1])
                        best = this if best is None else jnp.where(skip == k, this, best)
                    lanes_out.append(best)
                halves.append(jnp.concatenate(lanes_out, 1))
            real, imag = halves
            patch[0, top : top + CHUNK, :] = real
            patch[1, top : top + CHUNK, :] = imag
            p_re = probe[0, top : top + CHUNK, :]
            p_im = probe[1, top : top + CHUNK, :]
            waves[top : top + CHUNK, :] = (p_re * real - p_im * imag).astype(jnp.bfloat16)
            waves[wave + top : wave + top + CHUNK, :] = (p_re * imag + p_im * real).astype(
                jnp.bfloat16
            )

        sectioned = dot(table_a[...], waves[...]).astype(jnp.bfloat16)
        sections[:, :wave] = sectioned[:wave]
        sections[:, wave:] = sectioned[wave:]
        field[...] = dot(sections[...], table_b[...])

        for top in range(0, wave, CHUNK):
            real = field[top : top + CHUNK, :wave]
            imag = field[top : top + CHUNK, wave:]
            power = real * real + imag * imag
            measured = amps[0, 0, slot, top : top + CHUNK, :].astype(jnp.float32)
            factor = (measured * lax.rsqrt(power + 0.25) - 1.0) * live
            waves[top : top + CHUNK, :] = (real * factor).astype(jnp.bfloat16)
            waves[wave + top : wave + top + CHUNK, :] = (imag * factor).astype(jnp.bfloat16)

        sectioned = dot(table_b[...], waves[...]).astype(jnp.bfloat16)
        sections[:, :wave] = sectioned[:wave]
        sections[:, wave:] = sectioned[wave:]
        field[...] = dot(sections[...], table_a[...])

        for top in range(0, wave, CHUNK):
            real = field[top : top + CHUNK, :wave]
            imag = field[top : top + CHUNK, wave:]
            p_re = probe[0, top : top + CHUNK, :]
            p_im = probe[1, top : top + CHUNK, :]
            w_re = patch[0, top : top + CHUNK, :]
            w_im = patch[1, top : top + CHUNK, :]
            probe_grad[0, top : top + CHUNK, :] += w_re * real + w_im * imag
            probe_grad[1, top : top + CHUNK, :] += w_re * imag - w_im * real
            steps = (p_re * real + p_im * imag, p_re * imag - p_im * real)
            for part in range(2):
                turned = [
                    pltpu.roll(steps[part][:, w * LANES : (w + 1) * LANES], ahead, 1)
                    for w in range(wide)
                ]
                zero = jnp.zeros((CHUNK, LANES), jnp.float32)

                def block(index):
                    return turned[index] if 0 <= index < wide else zero

                for p in range(pieces):
                    best = None
                    for k in range(pieces - wide + 1):
                        this = jnp.where(high, block(p - k), block(p - k - 1))
                        best = this if best is None else jnp.where(skip == k, this, best)
                    terms[part, p, pl.ds(row + top, CHUNK), :] += best
        return carry

    lax.fori_loop(0, slots, slot_step, 0)
    for part in range(2):
        for p in range(pieces):
            grad[part, :, p * LANES : (p + 1) * LANES] = terms[part, p]


def scan_terms(anchors, jitter, counts, padded, probe, amps, table_a, table_b):
    wave = amps.shape[3]
    _, extent, columns = padded.shape
    blocks = pltpu.VMEM((2, columns // LANES, extent, LANES), jnp.float32)
    vmem = pl.BlockSpec(memory_space=pltpu.VMEM)
    smem = pl.BlockSpec(memory_space=pltpu.SMEM)
    return pl.pallas_call(
        scan_kernel,
        out_shape=(
            jax.ShapeDtypeStruct(padded.shape, jnp.float32),
            jax.ShapeDtypeStruct(probe.shape, jnp.float32),
        ),
        in_specs=[smem, smem, smem, vmem, vmem, vmem, vmem, vmem],
        out_specs=(vmem, vmem),
        scratch_shapes=[
            blocks,
            blocks,
            pltpu.VMEM((2, wave, wave), jnp.float32),
            pltpu.VMEM((2 * wave, wave), jnp.bfloat16),
            pltpu.VMEM((wave, 2 * wave), jnp.bfloat16),
            pltpu.VMEM((wave, 2 * wave), jnp.float32),
        ],
        compiler_params=pltpu.CompilerParams(vmem_limit_bytes=32 * 1024 * 1024),
        name="scan_terms",
    )(anchors, jitter, counts, padded, probe, amps, table_a, table_b)


class Links:
    def __init__(self, send, recv, n_tile, n_scan):
        self.send, self.recv = send, recv
        self.used = 0
        self.drain = []
        self.n_tile = n_tile
        self.chips = n_scan // CORES
        self.tile = lax.axis_index("tile")
        self.scan = lax.axis_index("scan")
        self.chip = self.scan // CORES
        self.core = self.scan % CORES

    def other_core(self):
        return {"scan": self.chip * CORES + 1 - self.core}

    def chip_at(self, step):
        return (self.chip + step) % self.chips

    def on_chip(self, step):
        return {"scan": self.chip_at(step) * CORES + self.core}

    def greet(self, tiles):
        barrier = pltpu.get_barrier_semaphore()
        peers = [self.other_core()] + [self.on_chip(k) for k in range(1, self.chips)]
        peers += [{"tile": (self.tile + k) % self.n_tile} for k in tiles]
        for peer in peers:
            pl.semaphore_signal(
                barrier, inc=1, device_id=peer, device_id_type=pl.DeviceIdType.MESH
            )
        pl.semaphore_wait(barrier, len(peers))

    def copy(self, source, target, device, when=None):
        made = pltpu.make_async_remote_copy(
            src_ref=source,
            dst_ref=target,
            send_sem=self.send.at[self.used],
            recv_sem=self.recv.at[self.used],
            device_id=device,
            device_id_type=pl.DeviceIdType.MESH,
        )
        self.used += 1
        if when is None:
            made.start()
        else:
            pl.when(when)(made.start)
        self.drain.append((made, when))
        return made

    def finish(self):
        for made, when in self.drain:
            if when is None:
                made.wait_send()
            else:
                pl.when(when)(made.wait_send)


def on(when, action):
    if when is None:
        action()
    else:
        pl.when(when)(action)


def rim_kernel(n_tile, n_scan, wave, parts, own, padded, send, recv, stay):
    links = Links(send, recv, n_tile, n_scan)
    rows = own.shape[1]
    chips, tile, core, chip = links.chips, links.tile, links.core, links.chip
    share = wave // chips
    some = share // parts
    above, below = tile > 0, tile < n_tile - 1
    links.greet(sorted({1, n_tile - 1}))

    def at(owner, part, base):
        return pl.ds(base + owner * share + part * some, some)

    up = {"tile": (tile + n_tile - 1) % n_tile}
    first = [
        links.copy(own.at[core, at(chip, p, 0)], padded.at[core, at(chip, p, rows)], up, above)
        for p in range(parts)
    ]
    local = pltpu.make_async_copy(own, padded.at[:, pl.ds(0, rows)], stay)
    local.start()

    @pl.when(tile == n_tile - 1)
    def _():
        padded[:, rows:, :] = jnp.zeros((2, wave, own.shape[2]), jnp.float32)

    across, landed = [], []
    for p in range(parts):
        on(below, first[p].wait_recv)
        here = padded.at[core, at(chip, p, rows)]
        for k in range(1, chips):
            across.append((k, p, links.copy(here, here, links.on_chip(k), below)))
        landed.append(links.copy(here, here, links.other_core(), below))
    for k, p, made in across:
        on(below, made.wait_recv)
        here = padded.at[core, at(links.chip_at(chips - k), p, rows)]
        landed.append(links.copy(here, here, links.other_core(), below))
    for made in landed:
        on(below, made.wait_recv)
    local.wait()
    links.finish()


def merge_kernel(
    n_tile, n_scan, parts, scale, last, grad, probe_grad, old, probe, out, probe_out,
    core_in, core_probe, total, probe_total, chip_in, probe_in, rim_back, probe_parts,
    send, recv,
):
    links = Links(send, recv, n_tile, n_scan)
    chips, tile, core, chip = links.chips, links.tile, links.core, links.chip
    wave = probe.shape[1]
    rows = grad.shape[1] - wave
    rest = rows - wave
    head, some = wave // chips, wave // parts
    owners = probe_parts_of(n_tile, chips, wave)
    fine = head // owners
    above, below = tile > 0, tile < n_tile - 1
    down = {"tile": (tile + 1) % n_tile}
    up = {"tile": (tile + n_tile - 1) % n_tile}
    links.greet(range(1, n_tile))
    other = 1 - core
    partner = links.other_core()
    others = range(1, chips)
    spans = [pl.ds(p * some, some) for p in range(parts)]
    rims = [pl.ds(rows + p * some, some) for p in range(parts)]

    def to_core(span):
        return links.copy(grad.at[other, span], core_in.at[span], partner)

    got_probe = links.copy(probe_grad.at[other], core_probe, partner)
    got_rims = [to_core(span) for span in rims]
    got_tail = to_core(pl.ds(wave, rest))
    got_head = to_core(pl.ds(0, wave))

    got_probe.wait_recv()
    probe_total[...] = probe_grad[core] + core_probe[...]
    probe_sent = []
    for k in others:
        piece = probe_total.at[pl.ds(links.chip_at(k) * head, head)]
        probe_sent.append(links.copy(piece, probe_in.at[chip], links.on_chip(k)))

    rims_sent = []
    for got, span, landing in zip(got_rims, rims, spans):
        got.wait_recv()
        total[span, :] = grad[core, span, :] + core_in[span, :]
        rims_sent.append(links.copy(total.at[span], rim_back.at[landing], down, below))

    def to_chips(span):
        return [
            links.copy(total.at[span], chip_in.at[chip, span], links.on_chip(k)) for k in others
        ]

    tail_rows = pl.ds(wave, rest)
    got_tail.wait_recv()
    total[tail_rows, :] = grad[core, tail_rows, :] + core_in[tail_rows, :]
    tail_sent = to_chips(tail_rows)

    inverse = RATE / (
        jnp.max(probe[0] * probe[0] + probe[1] * probe[1], axis=(0, 1), keepdims=True) + 1e-06
    )
    got_head.wait_recv()

    def owns(index):
        return None if owners == n_tile else index < owners

    def owned(index):
        return index if owners == n_tile else jnp.minimum(index, owners - 1)

    head_sent, spread = [], []
    for p, (span, made) in enumerate(zip(spans, rims_sent)):
        on(above, made.wait_recv)
        back = jnp.where(above, rim_back[span, :], 0.0)
        total[span, :] = grad[core, span, :] + core_in[span, :] + back
        head_sent.append(to_chips(span))
        if p == 0:
            for made in probe_sent:
                made.wait_recv()
            mine = pl.ds(chip * head, head)
            whole = probe_total[mine, :]
            for k in others:
                whole = whole + probe_in[links.chip_at(k)]
            probe_total[mine, :] = whole
            for k in range(1, n_tile):
                to = (tile + k) % n_tile
                piece = probe_total.at[pl.ds(chip * head + owned(to) * fine, fine)]
                spread.append(links.copy(piece, probe_parts.at[tile], {"tile": to}, owns(to)))

    own_rows = pl.ds(chip * head + owned(tile) * fine, fine)
    for made in spread:
        on(owns(tile), made.wait_recv)

    def close():
        whole = probe_total[own_rows, :]
        for k in range(1, n_tile):
            whole = whole + probe_parts[(tile + k) % n_tile]
        probe_out[core, own_rows, :] = probe[core, own_rows, :] + whole * scale

    on(owns(tile), close)
    place = probe_out.at[core, own_rows]
    probe_back = [
        links.copy(place, place, {"tile": (tile + k) % n_tile}, owns(tile))
        for k in range(1, n_tile)
    ]
    landed = []

    def update(span, sent):
        for made in sent:
            made.wait_recv()
        if chips == 2:
            whole = total[span, :] + chip_in[1 - chip, span, :]
        else:
            whole = None
            for k in range(chips):
                term = jnp.where(chip == k, total[span, :], chip_in[k, span, :])
                whole = term if whole is None else whole + term
        out[core, span, :] = old[core, span, :] + inverse * whole
        here = out.at[core, span]
        landed.append((links.copy(here, here, partner), None))

    update(tail_rows, tail_sent)

    for k, made in zip(range(1, n_tile), probe_back):
        on(owns((tile + n_tile - k) % n_tile), made.wait_recv)
    here = probe_out.at[core, pl.ds(chip * head, head)]
    probe_across = [links.copy(here, here, links.on_chip(k)) for k in others]
    landed.append((links.copy(here, here, partner), None))

    rims_back = []
    for span, rim, sent in zip(spans, rims, head_sent):
        update(span, sent)
        if not last:
            rims_back.append(links.copy(out.at[core, span], out.at[core, rim], up, above))
    for k in others:
        probe_across[k - 1].wait_recv()
        here = probe_out.at[core, pl.ds(links.chip_at(chips - k) * head, head)]
        landed.append((links.copy(here, here, partner), None))
    if not last:

        @pl.when(tile == n_tile - 1)
        def _():
            out[:, rows:, :] = jnp.zeros((2, wave, out.shape[2]), jnp.float32)

        for rim, made in zip(rims, rims_back):
            on(below, made.wait_recv)
            here = out.at[core, rim]
            landed.append((links.copy(here, here, partner, below), below))
    for made, when in landed:
        on(when, made.wait_recv)
    links.finish()


def probe_parts_of(n_tile, chips, wave):
    owners = n_tile
    while (wave // chips) % owners or (wave // chips // owners) % 8:
        owners -= 1
    return owners


def first_rim(own, wave):
    n_tile, n_scan = lax.axis_size("tile"), lax.axis_size("scan")
    _, rows, columns = own.shape
    vmem = pl.BlockSpec(memory_space=pltpu.VMEM)
    parts = 4
    copies = parts * (2 * (n_scan // CORES) + 1)
    return pl.pallas_call(
        functools.partial(rim_kernel, n_tile, n_scan, wave, parts),
        out_shape=jax.ShapeDtypeStruct((2, rows + wave, columns), jnp.float32),
        in_specs=[pl.BlockSpec(memory_space=pltpu.HBM)],
        out_specs=vmem,
        scratch_shapes=[
            pltpu.SemaphoreType.DMA((copies,)),
            pltpu.SemaphoreType.DMA((copies,)),
            pltpu.SemaphoreType.DMA,
        ],
        compiler_params=pltpu.CompilerParams(
            collective_id=0, has_side_effects=True, vmem_limit_bytes=24 * 1024 * 1024
        ),
        name="first_rim",
    )(own)


def merge(grad, probe_grad, old, probe, scale, last, number):
    n_tile, n_scan = lax.axis_size("tile"), lax.axis_size("scan")
    chips = n_scan // CORES
    _, wave, _ = probe.shape
    _, extent, columns = grad.shape
    rows = extent - wave
    head = wave // chips
    fine = head // probe_parts_of(n_tile, chips, wave)
    vmem = pl.BlockSpec(memory_space=pltpu.VMEM)
    parts = 4
    copies = 8 + (5 + parts) * chips + 2 * n_tile + 5 * parts
    return pl.pallas_call(
        functools.partial(merge_kernel, n_tile, n_scan, parts, scale, last),
        out_shape=(
            jax.ShapeDtypeStruct((2, rows if last else extent, columns), jnp.float32),
            jax.ShapeDtypeStruct(probe.shape, jnp.float32),
        ),
        in_specs=[vmem] * 4,
        out_specs=(vmem, vmem),
        scratch_shapes=[
            pltpu.VMEM((extent, columns), jnp.float32),
            pltpu.VMEM((wave, wave), jnp.float32),
            pltpu.VMEM((extent, columns), jnp.float32),
            pltpu.VMEM((wave, wave), jnp.float32),
            pltpu.VMEM((chips, rows, columns), jnp.float32),
            pltpu.VMEM((chips, head, wave), jnp.float32),
            pltpu.VMEM((wave, columns), jnp.float32),
            pltpu.VMEM((n_tile, fine, wave), jnp.float32),
            pltpu.SemaphoreType.DMA((copies,)),
            pltpu.SemaphoreType.DMA((copies,)),
        ],
        compiler_params=pltpu.CompilerParams(
            collective_id=number, has_side_effects=True, vmem_limit_bytes=32 * 1024 * 1024
        ),
        name="merge_last" if last else "merge",
    )(grad, probe_grad, old, probe)


def body(object_field, probe_field, amplitudes, anchors, jitter, counts):
    wave = probe_field.shape[1]
    slots = amplitudes.shape[2]
    table_a, table_b = tables(wave)
    total_scans = slots * lax.axis_size("tile") * lax.axis_size("scan")
    scale = 1.0 / math.sqrt(total_scans)
    padded = first_rim(object_field, wave)
    probe = probe_field
    for iteration in range(ITERS):
        last = iteration == ITERS - 1
        grad, probe_grad = scan_terms(
            anchors, jitter, counts, padded, probe, amplitudes, table_a, table_b
        )
        padded, probe = merge(grad, probe_grad, padded, probe, scale, last, 1 + iteration)
    return (padded, probe)


def solution(mesh):
    in_specs = (
        P(None, ("groups", "tile"), None),
        P(None, "groups", None),
        P(("groups", "tile"), "scan", None, None, None),
        P(("groups", "tile"), "scan", None, None),
        P(("groups", "tile"), "scan", None, None),
        P(("groups", "tile"), "scan"),
    )
    out_specs = (P(None, ("groups", "tile"), None), P(None, "groups", None))
    return jax.shard_map(body, mesh=mesh, in_specs=in_specs, out_specs=out_specs, check_vma=False)
```

```python
import functools
import math

import jax
import jax.numpy as jnp
import numpy as np
from jax import lax
from jax.experimental import pallas as pl
from jax.experimental.pallas import tpu as pltpu
from jax.sharding import PartitionSpec as P

ITERS = 2
RATE = 0.25
CORES = 2
LANES = 128
CHUNK = 32


def tables(wave):
    index = np.arange(wave)
    angles = (index[:, None] * index[None, :] % wave) * (2.0 * math.pi / wave)
    cosine = np.cos(angles) / math.sqrt(wave)
    sines = np.sin(angles) / math.sqrt(wave)
    table_a = np.block([[cosine, sines], [-sines, cosine]])
    table_b = np.block([[cosine, -sines], [sines, cosine]])
    return (jnp.asarray(table_a, jnp.bfloat16), jnp.asarray(table_b, jnp.bfloat16))


def scan_kernel(
    starts, counts, padded, probe, amps, table_a, table_b, grad, probe_grad,
    window, terms, patches, waves_all, sections_all, fields,
):
    slots, wave = amps.shape[2:4]
    columns = padded.shape[2]
    pieces = columns // LANES
    wide = wave // LANES
    lane = lax.broadcasted_iota(jnp.int32, (CHUNK, LANES), 1)

    for part in range(2):
        for p in range(pieces):
            window[part, p] = padded[part, :, p * LANES : (p + 1) * LANES]
    terms[...] = jnp.zeros(terms.shape, jnp.float32)
    probe_grad[...] = jnp.zeros(probe_grad.shape, jnp.float32)

    def dot(left, right):
        return jnp.dot(left, right, preferred_element_type=jnp.float32)

    def slot_step(slot):
        patch, waves = patches.at[slot], waves_all.at[slot]
        sections, field = sections_all.at[slot], fields.at[slot]
        row = starts[slot, 0]
        col = starts[slot, 1]
        live = jnp.where(slot < counts[0, 0], 1.0, 0.0).astype(jnp.float32)
        back = lax.rem(LANES - col, LANES)
        ahead = lax.rem(col, LANES)
        low = lane < LANES - col
        high = lane >= col

        for top in range(0, wave, CHUNK):
            halves = []
            for part in range(2):
                turned = [
                    pltpu.roll(
                        window[part, p, pl.ds(row + top, CHUNK), :], back, 1
                    )
                    for p in range(pieces)
                ]
                lanes_out = [jnp.where(low, turned[w], turned[w + 1]) for w in range(wide)]
                halves.append(jnp.concatenate(lanes_out, 1))
            real, imag = halves
            patch[0, top : top + CHUNK, :] = real
            patch[1, top : top + CHUNK, :] = imag
            p_re = probe[0, top : top + CHUNK, :]
            p_im = probe[1, top : top + CHUNK, :]
            waves[top : top + CHUNK, :] = (p_re * real - p_im * imag).astype(jnp.bfloat16)
            waves[wave + top : wave + top + CHUNK, :] = (p_re * imag + p_im * real).astype(
                jnp.bfloat16
            )

        yield
        sectioned = dot(table_a[...], waves[...]).astype(jnp.bfloat16)
        sections[:, :wave] = sectioned[:wave]
        sections[:, wave:] = sectioned[wave:]
        field[...] = dot(sections[...], table_b[...])
        yield

        for top in range(0, wave, CHUNK):
            real = field[top : top + CHUNK, :wave]
            imag = field[top : top + CHUNK, wave:]
            power = real * real + imag * imag
            measured = amps[0, 0, slot, top : top + CHUNK, :].astype(jnp.float32)
            factor = (measured * lax.rsqrt(power + 0.25) - 1.0) * live
            waves[top : top + CHUNK, :] = (real * factor).astype(jnp.bfloat16)
            waves[wave + top : wave + top + CHUNK, :] = (imag * factor).astype(jnp.bfloat16)

        yield
        sectioned = dot(table_b[...], waves[...]).astype(jnp.bfloat16)
        sections[:, :wave] = sectioned[:wave]
        sections[:, wave:] = sectioned[wave:]
        field[...] = dot(sections[...], table_a[...])
        yield

        for top in range(0, wave, CHUNK):
            real = field[top : top + CHUNK, :wave]
            imag = field[top : top + CHUNK, wave:]
            p_re = probe[0, top : top + CHUNK, :]
            p_im = probe[1, top : top + CHUNK, :]
            w_re = patch[0, top : top + CHUNK, :]
            w_im = patch[1, top : top + CHUNK, :]
            probe_grad[0, top : top + CHUNK, :] += w_re * real + w_im * imag
            probe_grad[1, top : top + CHUNK, :] += w_re * imag - w_im * real
            steps = (p_re * real + p_im * imag, p_re * imag - p_im * real)
            for part in range(2):
                turned = [
                    pltpu.roll(steps[part][:, w * LANES : (w + 1) * LANES], ahead, 1)
                    for w in range(wide)
                ]
                zero = jnp.zeros((CHUNK, LANES), jnp.float32)
                ends = [zero] + turned + [zero]
                for p in range(pieces):
                    terms[part, p, pl.ds(row + top, CHUNK), :] += jnp.where(
                        high, ends[p + 1], ends[p]
                    )

    waiting = [slot_step(slot) for slot in range(slots)]
    active = []
    while waiting or active:
        if waiting:
            active.append(waiting.pop(0))
        active = [one for one in active if next(one, active) is None]
    for part in range(2):
        for p in range(pieces):
            grad[part, :, p * LANES : (p + 1) * LANES] = terms[part, p]


def scan_terms(starts, counts, padded, probe, amps, table_a, table_b):
    slots, wave = amps.shape[2:4]
    _, extent, columns = padded.shape
    blocks = pltpu.VMEM((2, columns // LANES, extent, LANES), jnp.float32)
    vmem = pl.BlockSpec(memory_space=pltpu.VMEM)
    smem = pl.BlockSpec(memory_space=pltpu.SMEM)
    return pl.pallas_call(
        scan_kernel,
        out_shape=(
            jax.ShapeDtypeStruct(padded.shape, jnp.float32),
            jax.ShapeDtypeStruct(probe.shape, jnp.float32),
        ),
        in_specs=[smem, smem, vmem, vmem, vmem, vmem, vmem],
        out_specs=(vmem, vmem),
        scratch_shapes=[
            blocks,
            blocks,
            pltpu.VMEM((slots, 2, wave, wave), jnp.float32),
            pltpu.VMEM((slots, 2 * wave, wave), jnp.bfloat16),
            pltpu.VMEM((slots, wave, 2 * wave), jnp.bfloat16),
            pltpu.VMEM((slots, wave, 2 * wave), jnp.float32),
        ],
        compiler_params=pltpu.CompilerParams(vmem_limit_bytes=32 * 1024 * 1024),
        name="scan_terms",
    )(starts, counts, padded, probe, amps, table_a, table_b)


class Links:
    def __init__(self, send, recv, n_tile, n_scan):
        self.send, self.recv = send, recv
        self.used = 0
        self.drain = []
        self.n_tile = n_tile
        self.chips = n_scan // CORES
        self.tile = lax.axis_index("tile")
        self.scan = lax.axis_index("scan")
        self.chip = self.scan // CORES
        self.core = self.scan % CORES

    def other_core(self):
        return {"scan": self.chip * CORES + 1 - self.core}

    def chip_at(self, step):
        return (self.chip + step) % self.chips

    def on_chip(self, step):
        return {"scan": self.chip_at(step) * CORES + self.core}

    def greet(self, tiles):
        barrier = pltpu.get_barrier_semaphore()
        peers = [self.other_core()] + [self.on_chip(k) for k in range(1, self.chips)]
        peers += [{"tile": (self.tile + k) % self.n_tile} for k in tiles]
        for peer in peers:
            pl.semaphore_signal(
                barrier, inc=1, device_id=peer, device_id_type=pl.DeviceIdType.MESH
            )
        pl.semaphore_wait(barrier, len(peers))

    def copy(self, source, target, device, when=None):
        made = pltpu.make_async_remote_copy(
            src_ref=source,
            dst_ref=target,
            send_sem=self.send.at[self.used],
            recv_sem=self.recv.at[self.used],
            device_id=device,
            device_id_type=pl.DeviceIdType.MESH,
        )
        self.used += 1
        if when is None:
            made.start()
        else:
            pl.when(when)(made.start)
        self.drain.append((made, when))
        return made

    def finish(self):
        for made, when in self.drain:
            if when is None:
                made.wait_send()
            else:
                pl.when(when)(made.wait_send)


def on(when, action):
    if when is None:
        action()
    else:
        pl.when(when)(action)


def rim_kernel(n_tile, n_scan, wave, parts, own, padded, send, recv, stay):
    links = Links(send, recv, n_tile, n_scan)
    rows = own.shape[1]
    chips, tile, core, chip = links.chips, links.tile, links.core, links.chip
    share = wave // chips
    some = share // parts
    above, below = tile > 0, tile < n_tile - 1
    links.greet(sorted({1, n_tile - 1}))

    def at(owner, part, base):
        return pl.ds(base + owner * share + part * some, some)

    up = {"tile": (tile + n_tile - 1) % n_tile}
    first = [
        links.copy(own.at[core, at(chip, p, 0)], padded.at[core, at(chip, p, rows)], up, above)
        for p in range(parts)
    ]
    local = pltpu.make_async_copy(own, padded.at[:, pl.ds(0, rows)], stay)
    local.start()

    @pl.when(tile == n_tile - 1)
    def _():
        padded[:, rows:, :] = jnp.zeros((2, wave, own.shape[2]), jnp.float32)

    across, landed = [], []
    for p in range(parts):
        on(below, first[p].wait_recv)
        here = padded.at[core, at(chip, p, rows)]
        for k in range(1, chips):
            across.append((k, p, links.copy(here, here, links.on_chip(k), below)))
        landed.append(links.copy(here, here, links.other_core(), below))
    for k, p, made in across:
        on(below, made.wait_recv)
        here = padded.at[core, at(links.chip_at(chips - k), p, rows)]
        landed.append(links.copy(here, here, links.other_core(), below))
    for made in landed:
        on(below, made.wait_recv)
    local.wait()
    links.finish()


def merge_kernel(
    n_tile, n_scan, parts, scale, last, grad, probe_grad, old, probe, out, probe_out,
    core_in, core_probe, total, probe_total, chip_in, probe_in, rim_back, probe_parts,
    send, recv,
):
    links = Links(send, recv, n_tile, n_scan)
    chips, tile, core, chip = links.chips, links.tile, links.core, links.chip
    wave = probe.shape[1]
    rows = grad.shape[1] - wave
    rest = rows - wave
    head, some = wave // chips, wave // parts
    owners = probe_parts_of(n_tile, chips, wave)
    fine = head // owners
    above, below = tile > 0, tile < n_tile - 1
    down = {"tile": (tile + 1) % n_tile}
    up = {"tile": (tile + n_tile - 1) % n_tile}
    links.greet(range(1, n_tile))
    other = 1 - core
    partner = links.other_core()
    others = range(1, chips)
    spans = [pl.ds(p * some, some) for p in range(parts)]
    rims = [pl.ds(rows + p * some, some) for p in range(parts)]

    def to_core(span):
        return links.copy(grad.at[other, span], core_in.at[span], partner)

    got_probe = links.copy(probe_grad.at[other], core_probe, partner)
    got_rims = [to_core(span) for span in rims]
    got_tail = to_core(pl.ds(wave, rest))
    got_head = to_core(pl.ds(0, wave))

    got_probe.wait_recv()
    probe_total[...] = probe_grad[core] + core_probe[...]
    probe_sent = []
    for k in others:
        piece = probe_total.at[pl.ds(links.chip_at(k) * head, head)]
        probe_sent.append(links.copy(piece, probe_in.at[chip], links.on_chip(k)))

    rims_sent = []
    for got, span, landing in zip(got_rims, rims, spans):
        got.wait_recv()
        total[span, :] = grad[core, span, :] + core_in[span, :]
        rims_sent.append(links.copy(total.at[span], rim_back.at[landing], down, below))

    def to_chips(span):
        return [
            links.copy(total.at[span], chip_in.at[chip, span], links.on_chip(k)) for k in others
        ]

    tail_rows = pl.ds(wave, rest)
    got_tail.wait_recv()
    total[tail_rows, :] = grad[core, tail_rows, :] + core_in[tail_rows, :]
    early, late = pl.ds(wave, rest // 2), pl.ds(wave + rest // 2, rest // 2)
    early_sent = to_chips(early)

    inverse = RATE / (
        jnp.max(probe[0] * probe[0] + probe[1] * probe[1], axis=(0, 1), keepdims=True) + 1e-06
    )
    got_head.wait_recv()

    def owns(index):
        return None if owners == n_tile else index < owners

    def owned(index):
        return index if owners == n_tile else jnp.minimum(index, owners - 1)

    head_sent, spread = [], []
    for p, (span, made) in enumerate(zip(spans, rims_sent)):
        on(above, made.wait_recv)
        back = jnp.where(above, rim_back[span, :], 0.0)
        total[span, :] = grad[core, span, :] + core_in[span, :] + back
        head_sent.append(to_chips(span))
        if p == 0:
            for made in probe_sent:
                made.wait_recv()
            mine = pl.ds(chip * head, head)
            whole = probe_total[mine, :]
            for k in others:
                whole = whole + probe_in[links.chip_at(k)]
            probe_total[mine, :] = whole
            for k in range(1, n_tile):
                to = (tile + k) % n_tile
                piece = probe_total.at[pl.ds(chip * head + owned(to) * fine, fine)]
                spread.append(links.copy(piece, probe_parts.at[tile], {"tile": to}, owns(to)))

    late_sent = to_chips(late)

    own_rows = pl.ds(chip * head + owned(tile) * fine, fine)
    for made in spread:
        on(owns(tile), made.wait_recv)

    def close():
        whole = probe_total[own_rows, :]
        for k in range(1, n_tile):
            whole = whole + probe_parts[(tile + k) % n_tile]
        probe_out[core, own_rows, :] = probe[core, own_rows, :] + whole * scale

    on(owns(tile), close)
    place = probe_out.at[core, own_rows]
    probe_back = [
        links.copy(place, place, {"tile": (tile + k) % n_tile}, owns(tile))
        for k in range(1, n_tile)
    ]
    landed = []

    def update(span, sent):
        for made in sent:
            made.wait_recv()
        if chips == 2:
            whole = total[span, :] + chip_in[1 - chip, span, :]
        else:
            whole = None
            for k in range(chips):
                term = jnp.where(chip == k, total[span, :], chip_in[k, span, :])
                whole = term if whole is None else whole + term
        out[core, span, :] = old[core, span, :] + inverse * whole
        here = out.at[core, span]
        landed.append((links.copy(here, here, partner), None))

    update(early, early_sent)

    for k, made in zip(range(1, n_tile), probe_back):
        on(owns((tile + n_tile - k) % n_tile), made.wait_recv)
    here = probe_out.at[core, pl.ds(chip * head, head)]
    probe_across = [links.copy(here, here, links.on_chip(k)) for k in others]
    landed.append((links.copy(here, here, partner), None))

    rims_back = []
    for span, rim, sent in zip(spans, rims, head_sent):
        update(span, sent)
        if not last:
            rims_back.append(links.copy(out.at[core, span], out.at[core, rim], up, above))
    update(late, late_sent)
    for k in others:
        probe_across[k - 1].wait_recv()
        here = probe_out.at[core, pl.ds(links.chip_at(chips - k) * head, head)]
        landed.append((links.copy(here, here, partner), None))
    if not last:

        @pl.when(tile == n_tile - 1)
        def _():
            out[:, rows:, :] = jnp.zeros((2, wave, out.shape[2]), jnp.float32)

        for rim, made in zip(rims, rims_back):
            on(below, made.wait_recv)
            here = out.at[core, rim]
            landed.append((links.copy(here, here, partner, below), below))
    for made, when in landed:
        on(when, made.wait_recv)
    links.finish()


def probe_parts_of(n_tile, chips, wave):
    owners = n_tile
    while (wave // chips) % owners or (wave // chips // owners) % 8:
        owners -= 1
    return owners


def first_rim(own, wave):
    n_tile, n_scan = lax.axis_size("tile"), lax.axis_size("scan")
    _, rows, columns = own.shape
    vmem = pl.BlockSpec(memory_space=pltpu.VMEM)
    parts = 4
    copies = parts * (2 * (n_scan // CORES) + 1)
    return pl.pallas_call(
        functools.partial(rim_kernel, n_tile, n_scan, wave, parts),
        out_shape=jax.ShapeDtypeStruct((2, rows + wave, columns), jnp.float32),
        in_specs=[pl.BlockSpec(memory_space=pltpu.HBM)],
        out_specs=vmem,
        scratch_shapes=[
            pltpu.SemaphoreType.DMA((copies,)),
            pltpu.SemaphoreType.DMA((copies,)),
            pltpu.SemaphoreType.DMA,
        ],
        compiler_params=pltpu.CompilerParams(
            collective_id=0, has_side_effects=True, vmem_limit_bytes=24 * 1024 * 1024
        ),
        name="first_rim",
    )(own)


def merge(grad, probe_grad, old, probe, scale, last, number):
    n_tile, n_scan = lax.axis_size("tile"), lax.axis_size("scan")
    chips = n_scan // CORES
    _, wave, _ = probe.shape
    _, extent, columns = grad.shape
    rows = extent - wave
    head = wave // chips
    fine = head // probe_parts_of(n_tile, chips, wave)
    vmem = pl.BlockSpec(memory_space=pltpu.VMEM)
    parts = 4
    copies = 8 + (6 + parts) * chips + 2 * n_tile + 5 * parts
    return pl.pallas_call(
        functools.partial(merge_kernel, n_tile, n_scan, parts, scale, last),
        out_shape=(
            jax.ShapeDtypeStruct((2, rows if last else extent, columns), jnp.float32),
            jax.ShapeDtypeStruct(probe.shape, jnp.float32),
        ),
        in_specs=[vmem] * 4,
        out_specs=(vmem, vmem),
        scratch_shapes=[
            pltpu.VMEM((extent, columns), jnp.float32),
            pltpu.VMEM((wave, wave), jnp.float32),
            pltpu.VMEM((extent, columns), jnp.float32),
            pltpu.VMEM((wave, wave), jnp.float32),
            pltpu.VMEM((chips, rows, columns), jnp.float32),
            pltpu.VMEM((chips, head, wave), jnp.float32),
            pltpu.VMEM((wave, columns), jnp.float32),
            pltpu.VMEM((n_tile, fine, wave), jnp.float32),
            pltpu.SemaphoreType.DMA((copies,)),
            pltpu.SemaphoreType.DMA((copies,)),
        ],
        compiler_params=pltpu.CompilerParams(
            collective_id=number, has_side_effects=True, vmem_limit_bytes=32 * 1024 * 1024
        ),
        name="merge_last" if last else "merge",
    )(grad, probe_grad, old, probe)


def body(object_field, probe_field, amplitudes, anchors, jitter, counts):
    wave = probe_field.shape[1]
    slots = amplitudes.shape[2]
    table_a, table_b = tables(wave)
    starts = (anchors + jitter)[0, 0]
    total_scans = slots * lax.axis_size("tile") * lax.axis_size("scan")
    scale = 1.0 / math.sqrt(total_scans)
    padded = first_rim(object_field, wave)
    probe = probe_field
    for iteration in range(ITERS):
        last = iteration == ITERS - 1
        grad, probe_grad = scan_terms(
            starts, counts, padded, probe, amplitudes, table_a, table_b
        )
        padded, probe = merge(grad, probe_grad, padded, probe, scale, last, 1 + iteration)
    return (padded, probe)


def solution(mesh):
    in_specs = (
        P(None, ("groups", "tile"), None),
        P(None, "groups", None),
        P(("groups", "tile"), "scan", None, None, None),
        P(("groups", "tile"), "scan", None, None),
        P(("groups", "tile"), "scan", None, None),
        P(("groups", "tile"), "scan"),
    )
    out_specs = (P(None, ("groups", "tile"), None), P(None, "groups", None))
    return jax.shard_map(body, mesh=mesh, in_specs=in_specs, out_specs=out_specs, check_vma=False)
```

```python
import functools
import math

import jax
import jax.numpy as jnp
import numpy as np
from jax import lax
from jax.experimental import pallas as pl
from jax.experimental.pallas import tpu as pltpu
from jax.sharding import PartitionSpec as P

ITERS = 2
RATE = 0.25
CORES = 2
LANES = 128
CHUNK = 32


def tables(wave):
    index = np.arange(wave)
    angles = (index[:, None] * index[None, :] % wave) * (2.0 * math.pi / wave)
    cosine = np.cos(angles) / math.sqrt(wave)
    sines = np.sin(angles) / math.sqrt(wave)
    table_a = np.block([[cosine, sines], [-sines, cosine]])
    table_b = np.block([[cosine, -sines], [sines, cosine]])
    return (jnp.asarray(table_a, jnp.bfloat16), jnp.asarray(table_b, jnp.bfloat16))


def scan_kernel(
    starts, counts, padded, probe, amps, table_a, table_b, grad, probe_grad,
    window, terms, patches, waves_all, sections_all, fields,
):
    slots, wave = amps.shape[2:4]
    columns = padded.shape[2]
    pieces = columns // LANES
    wide = wave // LANES
    lane = lax.broadcasted_iota(jnp.int32, (CHUNK, LANES), 1)

    for part in range(2):
        for p in range(pieces):
            window[part, p] = padded[part, :, p * LANES : (p + 1) * LANES]
    terms[...] = jnp.zeros(terms.shape, jnp.float32)
    probe_grad[...] = jnp.zeros(probe_grad.shape, jnp.float32)

    def dot(left, right):
        return jnp.dot(left, right, preferred_element_type=jnp.float32)

    def slot_step(slot):
        patch, waves = patches.at[slot], waves_all.at[slot]
        sections, field = sections_all.at[slot], fields.at[slot]
        row = starts[slot, 0]
        col = starts[slot, 1]
        live = jnp.where(slot < counts[0, 0], 1.0, 0.0).astype(jnp.float32)
        back = lax.rem(LANES - col, LANES)
        ahead = lax.rem(col, LANES)
        low = lane < LANES - col
        high = lane >= col

        for top in range(0, wave, CHUNK):
            halves = []
            for part in range(2):
                turned = [
                    pltpu.roll(
                        window[part, p, pl.ds(row + top, CHUNK), :], back, 1
                    )
                    for p in range(pieces)
                ]
                lanes_out = [jnp.where(low, turned[w], turned[w + 1]) for w in range(wide)]
                halves.append(jnp.concatenate(lanes_out, 1))
            real, imag = halves
            patch[0, top : top + CHUNK, :] = real
            patch[1, top : top + CHUNK, :] = imag
            p_re = probe[0, top : top + CHUNK, :]
            p_im = probe[1, top : top + CHUNK, :]
            waves[top : top + CHUNK, :] = (p_re * real - p_im * imag).astype(jnp.bfloat16)
            waves[wave + top : wave + top + CHUNK, :] = (p_re * imag + p_im * real).astype(
                jnp.bfloat16
            )

        yield
        sectioned = dot(table_a[...], waves[...]).astype(jnp.bfloat16)
        sections[:, :wave] = sectioned[:wave]
        sections[:, wave:] = sectioned[wave:]
        field[...] = dot(sections[...], table_b[...])
        yield

        for top in range(0, wave, CHUNK):
            real = field[top : top + CHUNK, :wave]
            imag = field[top : top + CHUNK, wave:]
            power = real * real + imag * imag
            measured = amps[0, 0, slot, top : top + CHUNK, :].astype(jnp.float32)
            factor = (measured * lax.rsqrt(power + 0.25) - 1.0) * live
            waves[top : top + CHUNK, :] = (real * factor).astype(jnp.bfloat16)
            waves[wave + top : wave + top + CHUNK, :] = (imag * factor).astype(jnp.bfloat16)

        yield
        sectioned = dot(table_b[...], waves[...]).astype(jnp.bfloat16)
        sections[:, :wave] = sectioned[:wave]
        sections[:, wave:] = sectioned[wave:]
        field[...] = dot(sections[...], table_a[...])
        yield

        for top in range(0, wave, CHUNK):
            real = field[top : top + CHUNK, :wave]
            imag = field[top : top + CHUNK, wave:]
            p_re = probe[0, top : top + CHUNK, :]
            p_im = probe[1, top : top + CHUNK, :]
            w_re = patch[0, top : top + CHUNK, :]
            w_im = patch[1, top : top + CHUNK, :]
            probe_grad[0, top : top + CHUNK, :] += w_re * real + w_im * imag
            probe_grad[1, top : top + CHUNK, :] += w_re * imag - w_im * real
            steps = (p_re * real + p_im * imag, p_re * imag - p_im * real)
            for part in range(2):
                turned = [
                    pltpu.roll(steps[part][:, w * LANES : (w + 1) * LANES], ahead, 1)
                    for w in range(wide)
                ]
                zero = jnp.zeros((CHUNK, LANES), jnp.float32)
                ends = [zero] + turned + [zero]
                for p in range(pieces):
                    terms[part, p, pl.ds(row + top, CHUNK), :] += jnp.where(
                        high, ends[p + 1], ends[p]
                    )

    waiting = [slot_step(slot) for slot in range(slots)]
    active = []
    while waiting or active:
        if waiting:
            active.append(waiting.pop(0))
        active = [one for one in active if next(one, active) is None]
    for part in range(2):
        for p in range(pieces):
            grad[part, :, p * LANES : (p + 1) * LANES] = terms[part, p]


def scan_terms(starts, counts, padded, probe, amps, table_a, table_b):
    slots, wave = amps.shape[2:4]
    _, extent, columns = padded.shape
    blocks = pltpu.VMEM((2, columns // LANES, extent, LANES), jnp.float32)
    vmem = pl.BlockSpec(memory_space=pltpu.VMEM)
    smem = pl.BlockSpec(memory_space=pltpu.SMEM)
    return pl.pallas_call(
        scan_kernel,
        out_shape=(
            jax.ShapeDtypeStruct(padded.shape, jnp.float32),
            jax.ShapeDtypeStruct(probe.shape, jnp.float32),
        ),
        in_specs=[smem, smem, vmem, vmem, vmem, vmem, vmem],
        out_specs=(vmem, vmem),
        scratch_shapes=[
            blocks,
            blocks,
            pltpu.VMEM((slots, 2, wave, wave), jnp.float32),
            pltpu.VMEM((slots, 2 * wave, wave), jnp.bfloat16),
            pltpu.VMEM((slots, wave, 2 * wave), jnp.bfloat16),
            pltpu.VMEM((slots, wave, 2 * wave), jnp.float32),
        ],
        compiler_params=pltpu.CompilerParams(vmem_limit_bytes=32 * 1024 * 1024),
        name="scan_terms",
    )(starts, counts, padded, probe, amps, table_a, table_b)


class Links:
    def __init__(self, send, recv, n_tile, n_scan):
        self.send, self.recv = send, recv
        self.used = 0
        self.drain = []
        self.n_tile = n_tile
        self.chips = n_scan // CORES
        self.tile = lax.axis_index("tile")
        self.scan = lax.axis_index("scan")
        self.chip = self.scan // CORES
        self.core = self.scan % CORES

    def other_core(self):
        return {"scan": self.chip * CORES + 1 - self.core}

    def chip_at(self, step):
        return (self.chip + step) % self.chips

    def on_chip(self, step):
        return {"scan": self.chip_at(step) * CORES + self.core}

    def greet(self, tiles):
        barrier = pltpu.get_barrier_semaphore()
        peers = [self.other_core()] + [self.on_chip(k) for k in range(1, self.chips)]
        peers += [{"tile": (self.tile + k) % self.n_tile} for k in tiles]
        for peer in peers:
            pl.semaphore_signal(
                barrier, inc=1, device_id=peer, device_id_type=pl.DeviceIdType.MESH
            )
        pl.semaphore_wait(barrier, len(peers))

    def copy(self, source, target, device, when=None):
        made = pltpu.make_async_remote_copy(
            src_ref=source,
            dst_ref=target,
            send_sem=self.send.at[self.used],
            recv_sem=self.recv.at[self.used],
            device_id=device,
            device_id_type=pl.DeviceIdType.MESH,
        )
        self.used += 1
        if when is None:
            made.start()
        else:
            pl.when(when)(made.start)
        self.drain.append((made, when))
        return made

    def finish(self):
        for made, when in self.drain:
            if when is None:
                made.wait_send()
            else:
                pl.when(when)(made.wait_send)


def on(when, action):
    if when is None:
        action()
    else:
        pl.when(when)(action)


def rim_kernel(n_tile, n_scan, wave, parts, own, padded, send, recv, stay):
    links = Links(send, recv, n_tile, n_scan)
    rows = own.shape[1]
    chips, tile, core, chip = links.chips, links.tile, links.core, links.chip
    share = wave // chips
    some = share // parts
    above, below = tile > 0, tile < n_tile - 1
    links.greet(sorted({1, n_tile - 1}))

    def at(owner, part, base):
        return pl.ds(base + owner * share + part * some, some)

    up = {"tile": (tile + n_tile - 1) % n_tile}
    first = [
        links.copy(own.at[core, at(chip, p, 0)], padded.at[core, at(chip, p, rows)], up, above)
        for p in range(parts)
    ]
    local = pltpu.make_async_copy(own, padded.at[:, pl.ds(0, rows)], stay)
    local.start()

    @pl.when(tile == n_tile - 1)
    def _():
        padded[:, rows:, :] = jnp.zeros((2, wave, own.shape[2]), jnp.float32)

    across, landed = [], []
    for p in range(parts):
        on(below, first[p].wait_recv)
        here = padded.at[core, at(chip, p, rows)]
        for k in range(1, chips):
            across.append((k, p, links.copy(here, here, links.on_chip(k), below)))
        landed.append(links.copy(here, here, links.other_core(), below))
    for k, p, made in across:
        on(below, made.wait_recv)
        here = padded.at[core, at(links.chip_at(chips - k), p, rows)]
        landed.append(links.copy(here, here, links.other_core(), below))
    for made in landed:
        on(below, made.wait_recv)
    local.wait()
    links.finish()


def merge_kernel(
    n_tile, n_scan, parts, scale, last, grad, probe_grad, old, probe, out, probe_out,
    core_in, core_probe, total, probe_total, chip_in, probe_in, rim_back, probe_parts,
    send, recv,
):
    links = Links(send, recv, n_tile, n_scan)
    chips, tile, core, chip = links.chips, links.tile, links.core, links.chip
    wave = probe.shape[1]
    rows = grad.shape[1] - wave
    rest = rows - wave
    head, some = wave // chips, wave // parts
    owners = probe_parts_of(n_tile, chips, wave)
    fine = head // owners
    above, below = tile > 0, tile < n_tile - 1
    down = {"tile": (tile + 1) % n_tile}
    up = {"tile": (tile + n_tile - 1) % n_tile}
    links.greet(range(1, n_tile))
    other = 1 - core
    partner = links.other_core()
    others = range(1, chips)
    spans = [pl.ds(p * some, some) for p in range(parts)]
    rims = [pl.ds(rows + p * some, some) for p in range(parts)]

    def to_core(span):
        return links.copy(grad.at[other, span], core_in.at[span], partner)

    got_probe = links.copy(probe_grad.at[other], core_probe, partner)
    got_rims = [to_core(span) for span in rims]
    got_tail = to_core(pl.ds(wave, rest))
    got_head = to_core(pl.ds(0, wave))

    got_probe.wait_recv()
    probe_total[...] = probe_grad[core] + core_probe[...]
    probe_sent = []
    for k in others:
        piece = probe_total.at[pl.ds(links.chip_at(k) * head, head)]
        probe_sent.append(links.copy(piece, probe_in.at[chip], links.on_chip(k)))

    rims_sent = []
    for got, span, landing in zip(got_rims, rims, spans):
        got.wait_recv()
        total[span, :] = grad[core, span, :] + core_in[span, :]
        rims_sent.append(links.copy(total.at[span], rim_back.at[landing], down, below))

    def to_chips(span):
        return [
            links.copy(total.at[span], chip_in.at[chip, span], links.on_chip(k)) for k in others
        ]

    tail_rows = pl.ds(wave, rest)
    got_tail.wait_recv()
    total[tail_rows, :] = grad[core, tail_rows, :] + core_in[tail_rows, :]
    early, late = pl.ds(wave, rest // 2), pl.ds(wave + rest // 2, rest // 2)
    early_sent = to_chips(early)

    inverse = RATE / (
        jnp.max(probe[0] * probe[0] + probe[1] * probe[1], axis=(0, 1), keepdims=True) + 1e-06
    )
    got_head.wait_recv()

    def owns(index):
        return None if owners == n_tile else index < owners

    def owned(index):
        return index if owners == n_tile else jnp.minimum(index, owners - 1)

    head_sent, spread = [], []
    for p, (span, made) in enumerate(zip(spans, rims_sent)):
        on(above, made.wait_recv)
        back = jnp.where(above, rim_back[span, :], 0.0)
        total[span, :] = grad[core, span, :] + core_in[span, :] + back
        head_sent.append(to_chips(span))
        if p == 0:
            for made in probe_sent:
                made.wait_recv()
            mine = pl.ds(chip * head, head)
            whole = probe_total[mine, :]
            for k in others:
                whole = whole + probe_in[links.chip_at(k)]
            probe_total[mine, :] = whole
            for k in range(1, n_tile):
                to = (tile + k) % n_tile
                piece = probe_total.at[pl.ds(chip * head + owned(to) * fine, fine)]
                spread.append(links.copy(piece, probe_parts.at[tile], {"tile": to}, owns(to)))

    late_sent = to_chips(late)

    landed = []

    def update(span, sent):
        for made in sent:
            made.wait_recv()
        if chips == 2:
            whole = total[span, :] + chip_in[1 - chip, span, :]
        else:
            whole = None
            for k in range(chips):
                term = jnp.where(chip == k, total[span, :], chip_in[k, span, :])
                whole = term if whole is None else whole + term
        out[core, span, :] = old[core, span, :] + inverse * whole
        here = out.at[core, span]
        landed.append((links.copy(here, here, partner), None))

    rims_back = []

    def update_head(first, after):
        for p in range(first, after):
            update(spans[p], head_sent[p])
            if not last:
                rims_back.append(
                    links.copy(out.at[core, spans[p]], out.at[core, rims[p]], up, above)
                )

    update(early, early_sent)
    update_head(0, parts // 2)

    own_rows = pl.ds(chip * head + owned(tile) * fine, fine)
    for made in spread:
        on(owns(tile), made.wait_recv)

    def close():
        whole = probe_total[own_rows, :]
        for k in range(1, n_tile):
            whole = whole + probe_parts[(tile + k) % n_tile]
        probe_out[core, own_rows, :] = probe[core, own_rows, :] + whole * scale

    on(owns(tile), close)
    place = probe_out.at[core, own_rows]
    probe_back = [
        links.copy(place, place, {"tile": (tile + k) % n_tile}, owns(tile))
        for k in range(1, n_tile)
    ]

    update_head(parts // 2, parts)
    for k, made in zip(range(1, n_tile), probe_back):
        on(owns((tile + n_tile - k) % n_tile), made.wait_recv)
    here = probe_out.at[core, pl.ds(chip * head, head)]
    probe_across = [links.copy(here, here, links.on_chip(k)) for k in others]
    landed.append((links.copy(here, here, partner), None))
    update(late, late_sent)
    for k in others:
        probe_across[k - 1].wait_recv()
        here = probe_out.at[core, pl.ds(links.chip_at(chips - k) * head, head)]
        landed.append((links.copy(here, here, partner), None))
    if not last:

        @pl.when(tile == n_tile - 1)
        def _():
            out[:, rows:, :] = jnp.zeros((2, wave, out.shape[2]), jnp.float32)

        for rim, made in zip(rims, rims_back):
            on(below, made.wait_recv)
            here = out.at[core, rim]
            landed.append((links.copy(here, here, partner, below), below))
    for made, when in landed:
        on(when, made.wait_recv)
    links.finish()


def probe_parts_of(n_tile, chips, wave):
    owners = n_tile
    while (wave // chips) % owners or (wave // chips // owners) % 8:
        owners -= 1
    return owners


def first_rim(own, wave):
    n_tile, n_scan = lax.axis_size("tile"), lax.axis_size("scan")
    _, rows, columns = own.shape
    vmem = pl.BlockSpec(memory_space=pltpu.VMEM)
    parts = 4
    copies = parts * (2 * (n_scan // CORES) + 1)
    return pl.pallas_call(
        functools.partial(rim_kernel, n_tile, n_scan, wave, parts),
        out_shape=jax.ShapeDtypeStruct((2, rows + wave, columns), jnp.float32),
        in_specs=[pl.BlockSpec(memory_space=pltpu.HBM)],
        out_specs=vmem,
        scratch_shapes=[
            pltpu.SemaphoreType.DMA((copies,)),
            pltpu.SemaphoreType.DMA((copies,)),
            pltpu.SemaphoreType.DMA,
        ],
        compiler_params=pltpu.CompilerParams(
            collective_id=0, has_side_effects=True, vmem_limit_bytes=24 * 1024 * 1024
        ),
        name="first_rim",
    )(own)


def merge(grad, probe_grad, old, probe, scale, last, number):
    n_tile, n_scan = lax.axis_size("tile"), lax.axis_size("scan")
    chips = n_scan // CORES
    _, wave, _ = probe.shape
    _, extent, columns = grad.shape
    rows = extent - wave
    head = wave // chips
    fine = head // probe_parts_of(n_tile, chips, wave)
    vmem = pl.BlockSpec(memory_space=pltpu.VMEM)
    parts = 4
    copies = 8 + (6 + parts) * chips + 2 * n_tile + 5 * parts
    return pl.pallas_call(
        functools.partial(merge_kernel, n_tile, n_scan, parts, scale, last),
        out_shape=(
            jax.ShapeDtypeStruct((2, rows if last else extent, columns), jnp.float32),
            jax.ShapeDtypeStruct(probe.shape, jnp.float32),
        ),
        in_specs=[vmem] * 4,
        out_specs=(vmem, vmem),
        scratch_shapes=[
            pltpu.VMEM((extent, columns), jnp.float32),
            pltpu.VMEM((wave, wave), jnp.float32),
            pltpu.VMEM((extent, columns), jnp.float32),
            pltpu.VMEM((wave, wave), jnp.float32),
            pltpu.VMEM((chips, rows, columns), jnp.float32),
            pltpu.VMEM((chips, head, wave), jnp.float32),
            pltpu.VMEM((wave, columns), jnp.float32),
            pltpu.VMEM((n_tile, fine, wave), jnp.float32),
            pltpu.SemaphoreType.DMA((copies,)),
            pltpu.SemaphoreType.DMA((copies,)),
        ],
        compiler_params=pltpu.CompilerParams(
            collective_id=number, has_side_effects=True, vmem_limit_bytes=32 * 1024 * 1024
        ),
        name="merge_last" if last else "merge",
    )(grad, probe_grad, old, probe)


def body(object_field, probe_field, amplitudes, anchors, jitter, counts):
    wave = probe_field.shape[1]
    slots = amplitudes.shape[2]
    table_a, table_b = tables(wave)
    starts = (anchors + jitter)[0, 0]
    total_scans = slots * lax.axis_size("tile") * lax.axis_size("scan")
    scale = 1.0 / math.sqrt(total_scans)
    padded = first_rim(object_field, wave)
    probe = probe_field
    for iteration in range(ITERS):
        last = iteration == ITERS - 1
        grad, probe_grad = scan_terms(
            starts, counts, padded, probe, amplitudes, table_a, table_b
        )
        padded, probe = merge(grad, probe_grad, padded, probe, scale, last, 1 + iteration)
    return (padded, probe)


def solution(mesh):
    in_specs = (
        P(None, ("groups", "tile"), None),
        P(None, "groups", None),
        P(("groups", "tile"), "scan", None, None, None),
        P(("groups", "tile"), "scan", None, None),
        P(("groups", "tile"), "scan", None, None),
        P(("groups", "tile"), "scan"),
    )
    out_specs = (P(None, ("groups", "tile"), None), P(None, "groups", None))
    return jax.shard_map(body, mesh=mesh, in_specs=in_specs, out_specs=out_specs, check_vma=False)
```

```python
import functools
import math

import jax
import jax.numpy as jnp
import numpy as np
from jax import lax
from jax.experimental import pallas as pl
from jax.experimental.pallas import tpu as pltpu
from jax.sharding import PartitionSpec as P

ITERS = 2
RATE = 0.25
CORES = 2
LANES = 128
CHUNK = 32


def tables(wave):
    index = np.arange(wave)
    angles = (index[:, None] * index[None, :] % wave) * (2.0 * math.pi / wave)
    cosine = np.cos(angles) / math.sqrt(wave)
    sines = np.sin(angles) / math.sqrt(wave)
    table_a = np.block([[cosine, sines], [-sines, cosine]])
    table_b = np.block([[cosine, -sines], [sines, cosine]])
    return (jnp.asarray(table_a, jnp.bfloat16), jnp.asarray(table_b, jnp.bfloat16))


def scan_kernel(
    starts, counts, padded, probe, amps, table_a, table_b, grad, probe_grad,
    window, terms, patches, waves_all, sections_all, fields,
):
    slots, wave = amps.shape[2:4]
    columns = padded.shape[2]
    pieces = columns // LANES
    wide = wave // LANES
    lane = lax.broadcasted_iota(jnp.int32, (CHUNK, LANES), 1)

    for part in range(2):
        for p in range(pieces):
            window[part, p] = padded[part, :, p * LANES : (p + 1) * LANES]
    terms[...] = jnp.zeros(terms.shape, jnp.float32)
    probe_grad[...] = jnp.zeros(probe_grad.shape, jnp.float32)

    def dot(left, right):
        return jnp.dot(left, right, preferred_element_type=jnp.float32)

    def slot_step(slot):
        patch, waves = patches.at[slot], waves_all.at[slot]
        sections, field = sections_all.at[slot], fields.at[slot]
        row = starts[slot, 0]
        col = starts[slot, 1]
        live = jnp.where(slot < counts[0, 0], 1.0, 0.0).astype(jnp.float32)
        back = lax.rem(LANES - col, LANES)
        ahead = lax.rem(col, LANES)
        low = lane < LANES - col
        high = lane >= col

        for top in range(0, wave, CHUNK):
            halves = []
            for part in range(2):
                turned = [
                    pltpu.roll(
                        window[part, p, pl.ds(row + top, CHUNK), :], back, 1
                    )
                    for p in range(pieces)
                ]
                lanes_out = [jnp.where(low, turned[w], turned[w + 1]) for w in range(wide)]
                halves.append(jnp.concatenate(lanes_out, 1))
            real, imag = halves
            patch[0, top : top + CHUNK, :] = real
            patch[1, top : top + CHUNK, :] = imag
            p_re = probe[0, top : top + CHUNK, :]
            p_im = probe[1, top : top + CHUNK, :]
            waves[top : top + CHUNK, :] = (p_re * real - p_im * imag).astype(jnp.bfloat16)
            waves[wave + top : wave + top + CHUNK, :] = (p_re * imag + p_im * real).astype(
                jnp.bfloat16
            )

        yield
        sectioned = dot(table_a[...], waves[...]).astype(jnp.bfloat16)
        sections[:, :wave] = sectioned[:wave]
        sections[:, wave:] = sectioned[wave:]
        field[...] = dot(sections[...], table_b[...])
        yield

        for top in range(0, wave, CHUNK):
            real = field[top : top + CHUNK, :wave]
            imag = field[top : top + CHUNK, wave:]
            power = real * real + imag * imag
            measured = amps[0, 0, slot, top : top + CHUNK, :].astype(jnp.float32)
            factor = (measured * lax.rsqrt(power + 0.25) - 1.0) * live
            waves[top : top + CHUNK, :] = (real * factor).astype(jnp.bfloat16)
            waves[wave + top : wave + top + CHUNK, :] = (imag * factor).astype(jnp.bfloat16)

        yield
        sectioned = dot(table_b[...], waves[...]).astype(jnp.bfloat16)
        sections[:, :wave] = sectioned[:wave]
        sections[:, wave:] = sectioned[wave:]
        field[...] = dot(sections[...], table_a[...])
        yield

        for top in range(0, wave, CHUNK):
            real = field[top : top + CHUNK, :wave]
            imag = field[top : top + CHUNK, wave:]
            p_re = probe[0, top : top + CHUNK, :]
            p_im = probe[1, top : top + CHUNK, :]
            w_re = patch[0, top : top + CHUNK, :]
            w_im = patch[1, top : top + CHUNK, :]
            probe_grad[0, top : top + CHUNK, :] += w_re * real + w_im * imag
            probe_grad[1, top : top + CHUNK, :] += w_re * imag - w_im * real
            steps = (p_re * real + p_im * imag, p_re * imag - p_im * real)
            for part in range(2):
                turned = [
                    pltpu.roll(steps[part][:, w * LANES : (w + 1) * LANES], ahead, 1)
                    for w in range(wide)
                ]
                zero = jnp.zeros((CHUNK, LANES), jnp.float32)
                ends = [zero] + turned + [zero]
                for p in range(pieces):
                    terms[part, p, pl.ds(row + top, CHUNK), :] += jnp.where(
                        high, ends[p + 1], ends[p]
                    )

    waiting = [slot_step(slot) for slot in range(slots)]
    active = []
    while waiting or active:
        if waiting:
            active.append(waiting.pop(0))
        active = [one for one in active if next(one, active) is None]
    for part in range(2):
        for p in range(pieces):
            grad[part, :, p * LANES : (p + 1) * LANES] = terms[part, p]


def scan_terms(starts, counts, padded, probe, amps, table_a, table_b):
    slots, wave = amps.shape[2:4]
    _, extent, columns = padded.shape
    blocks = pltpu.VMEM((2, columns // LANES, extent, LANES), jnp.float32)
    vmem = pl.BlockSpec(memory_space=pltpu.VMEM)
    smem = pl.BlockSpec(memory_space=pltpu.SMEM)
    return pl.pallas_call(
        scan_kernel,
        out_shape=(
            jax.ShapeDtypeStruct(padded.shape, jnp.float32),
            jax.ShapeDtypeStruct(probe.shape, jnp.float32),
        ),
        in_specs=[smem, smem, vmem, vmem, vmem, vmem, vmem],
        out_specs=(vmem, vmem),
        scratch_shapes=[
            blocks,
            blocks,
            pltpu.VMEM((slots, 2, wave, wave), jnp.float32),
            pltpu.VMEM((slots, 2 * wave, wave), jnp.bfloat16),
            pltpu.VMEM((slots, wave, 2 * wave), jnp.bfloat16),
            pltpu.VMEM((slots, wave, 2 * wave), jnp.float32),
        ],
        compiler_params=pltpu.CompilerParams(vmem_limit_bytes=32 * 1024 * 1024),
        name="scan_terms",
    )(starts, counts, padded, probe, amps, table_a, table_b)


class Links:
    def __init__(self, send, recv, n_tile, n_scan):
        self.send, self.recv = send, recv
        self.used = 0
        self.drain = []
        self.n_tile = n_tile
        self.chips = n_scan // CORES
        self.tile = lax.axis_index("tile")
        self.scan = lax.axis_index("scan")
        self.chip = self.scan // CORES
        self.core = self.scan % CORES

    def other_core(self):
        return {"scan": self.chip * CORES + 1 - self.core}

    def chip_at(self, step):
        return (self.chip + step) % self.chips

    def on_chip(self, step):
        return {"scan": self.chip_at(step) * CORES + self.core}

    def greet(self, tiles):
        barrier = pltpu.get_barrier_semaphore()
        peers = [self.other_core()] + [self.on_chip(k) for k in range(1, self.chips)]
        peers += [{"tile": (self.tile + k) % self.n_tile} for k in tiles]
        for peer in peers:
            pl.semaphore_signal(
                barrier, inc=1, device_id=peer, device_id_type=pl.DeviceIdType.MESH
            )
        pl.semaphore_wait(barrier, len(peers))

    def copy(self, source, target, device, when=None):
        made = pltpu.make_async_remote_copy(
            src_ref=source,
            dst_ref=target,
            send_sem=self.send.at[self.used],
            recv_sem=self.recv.at[self.used],
            device_id=device,
            device_id_type=pl.DeviceIdType.MESH,
        )
        self.used += 1
        if when is None:
            made.start()
        else:
            pl.when(when)(made.start)
        self.drain.append((made, when))
        return made

    def finish(self):
        for made, when in self.drain:
            if when is None:
                made.wait_send()
            else:
                pl.when(when)(made.wait_send)


def on(when, action):
    if when is None:
        action()
    else:
        pl.when(when)(action)


def rim_kernel(n_tile, n_scan, wave, parts, own, padded, send, recv, stay):
    links = Links(send, recv, n_tile, n_scan)
    rows = own.shape[1]
    chips, tile, core, chip = links.chips, links.tile, links.core, links.chip
    share = wave // chips
    some = share // parts
    above, below = tile > 0, tile < n_tile - 1
    links.greet(sorted({1, n_tile - 1}))

    def at(owner, part, base):
        return pl.ds(base + owner * share + part * some, some)

    up = {"tile": (tile + n_tile - 1) % n_tile}
    first = [
        links.copy(own.at[core, at(chip, p, 0)], padded.at[core, at(chip, p, rows)], up, above)
        for p in range(parts)
    ]
    local = pltpu.make_async_copy(own, padded.at[:, pl.ds(0, rows)], stay)
    local.start()

    @pl.when(tile == n_tile - 1)
    def _():
        padded[:, rows:, :] = jnp.zeros((2, wave, own.shape[2]), jnp.float32)

    across, landed = [], []
    for p in range(parts):
        on(below, first[p].wait_recv)
        here = padded.at[core, at(chip, p, rows)]
        for k in range(1, chips):
            across.append((k, p, links.copy(here, here, links.on_chip(k), below)))
        landed.append(links.copy(here, here, links.other_core(), below))
    for k, p, made in across:
        on(below, made.wait_recv)
        here = padded.at[core, at(links.chip_at(chips - k), p, rows)]
        landed.append(links.copy(here, here, links.other_core(), below))
    for made in landed:
        on(below, made.wait_recv)
    local.wait()
    links.finish()


def merge_kernel(
    n_tile, n_scan, parts, scale, last, grad, probe_grad, old, probe, out, probe_out,
    core_in, core_probe, total, probe_total, chip_in, probe_in, rim_back, probe_parts,
    send, recv,
):
    links = Links(send, recv, n_tile, n_scan)
    chips, tile, core, chip = links.chips, links.tile, links.core, links.chip
    wave = probe.shape[1]
    rows = grad.shape[1] - wave
    rest = rows - wave
    head, some = wave // chips, wave // parts
    owners = probe_parts_of(n_tile, chips, wave)
    fine = head // owners
    above, below = tile > 0, tile < n_tile - 1
    down = {"tile": (tile + 1) % n_tile}
    up = {"tile": (tile + n_tile - 1) % n_tile}
    links.greet(range(1, n_tile))
    other = 1 - core
    partner = links.other_core()
    others = range(1, chips)
    spans = [pl.ds(p * some, some) for p in range(parts)]
    rims = [pl.ds(rows + p * some, some) for p in range(parts)]

    def to_core(span):
        return links.copy(grad.at[other, span], core_in.at[span], partner)

    got_probe = links.copy(probe_grad.at[other], core_probe, partner)
    got_rims = [to_core(span) for span in rims]
    got_tail = to_core(pl.ds(wave, rest))
    got_head = to_core(pl.ds(0, wave))

    got_probe.wait_recv()
    probe_total[...] = probe_grad[core] + core_probe[...]
    probe_sent = []
    for k in others:
        piece = probe_total.at[pl.ds(links.chip_at(k) * head, head)]
        probe_sent.append(links.copy(piece, probe_in.at[chip], links.on_chip(k)))

    def owns(index):
        return None if owners == n_tile else index < owners

    def owned(index):
        return index if owners == n_tile else jnp.minimum(index, owners - 1)

    def to_chips(span):
        return [
            links.copy(total.at[span], chip_in.at[chip, span], links.on_chip(k)) for k in others
        ]

    rims_sent = []

    def send_rims(first, after):
        for p in range(first, after):
            span = rims[p]
            got_rims[p].wait_recv()
            total[span, :] = grad[core, span, :] + core_in[span, :]
            rims_sent.append(links.copy(total.at[span], rim_back.at[spans[p]], down, below))

    head_sent = []

    def send_head(first, after):
        for p in range(first, after):
            span = spans[p]
            on(above, rims_sent[p].wait_recv)
            back = jnp.where(above, rim_back[span, :], 0.0)
            total[span, :] = grad[core, span, :] + core_in[span, :] + back
            head_sent.append(to_chips(span))

    landed = []

    def update(span, sent):
        for made in sent:
            made.wait_recv()
        if chips == 2:
            whole = total[span, :] + chip_in[1 - chip, span, :]
        else:
            whole = None
            for k in range(chips):
                term = jnp.where(chip == k, total[span, :], chip_in[k, span, :])
                whole = term if whole is None else whole + term
        out[core, span, :] = old[core, span, :] + inverse * whole
        here = out.at[core, span]
        landed.append((links.copy(here, here, partner), None))

    rims_back = []

    def update_head(first, after):
        for p in range(first, after):
            update(spans[p], head_sent[p])
            if not last:
                rims_back.append(
                    links.copy(out.at[core, spans[p]], out.at[core, rims[p]], up, above)
                )

    half = parts // 2
    send_rims(0, half)

    tail_rows = pl.ds(wave, rest)
    got_tail.wait_recv()
    total[tail_rows, :] = grad[core, tail_rows, :] + core_in[tail_rows, :]
    early, late = pl.ds(wave, rest // 2), pl.ds(wave + rest // 2, rest // 2)
    early_sent = to_chips(early)

    for made in probe_sent:
        made.wait_recv()
    mine = pl.ds(chip * head, head)
    whole = probe_total[mine, :]
    for k in others:
        whole = whole + probe_in[links.chip_at(k)]
    probe_total[mine, :] = whole
    spread = []
    for k in range(1, n_tile):
        to = (tile + k) % n_tile
        piece = probe_total.at[pl.ds(chip * head + owned(to) * fine, fine)]
        spread.append(links.copy(piece, probe_parts.at[tile], {"tile": to}, owns(to)))

    send_rims(half, parts)

    inverse = RATE / (
        jnp.max(probe[0] * probe[0] + probe[1] * probe[1], axis=(0, 1), keepdims=True) + 1e-06
    )
    got_head.wait_recv()

    send_head(0, half)
    late_sent = to_chips(late)
    update(early, early_sent)

    own_rows = pl.ds(chip * head + owned(tile) * fine, fine)
    for made in spread:
        on(owns(tile), made.wait_recv)

    def close():
        whole = probe_total[own_rows, :]
        for k in range(1, n_tile):
            whole = whole + probe_parts[(tile + k) % n_tile]
        probe_out[core, own_rows, :] = probe[core, own_rows, :] + whole * scale

    on(owns(tile), close)
    place = probe_out.at[core, own_rows]
    probe_back = [
        links.copy(place, place, {"tile": (tile + k) % n_tile}, owns(tile))
        for k in range(1, n_tile)
    ]

    for p in range(half, parts):
        update_head(p - half, p - half + 1)
        send_head(p, p + 1)
    update(late, late_sent)
    update_head(half, parts)
    for k, made in zip(range(1, n_tile), probe_back):
        on(owns((tile + n_tile - k) % n_tile), made.wait_recv)
    here = probe_out.at[core, pl.ds(chip * head, head)]
    probe_across = [links.copy(here, here, links.on_chip(k)) for k in others]
    landed.append((links.copy(here, here, partner), None))
    for k in others:
        probe_across[k - 1].wait_recv()
        here = probe_out.at[core, pl.ds(links.chip_at(chips - k) * head, head)]
        landed.append((links.copy(here, here, partner), None))
    if not last:

        @pl.when(tile == n_tile - 1)
        def _():
            out[:, rows:, :] = jnp.zeros((2, wave, out.shape[2]), jnp.float32)

        for rim, made in zip(rims, rims_back):
            on(below, made.wait_recv)
            here = out.at[core, rim]
            landed.append((links.copy(here, here, partner, below), below))
    for made, when in landed:
        on(when, made.wait_recv)
    links.finish()


def probe_parts_of(n_tile, chips, wave):
    owners = n_tile
    while (wave // chips) % owners or (wave // chips // owners) % 8:
        owners -= 1
    return owners


def first_rim(own, wave):
    n_tile, n_scan = lax.axis_size("tile"), lax.axis_size("scan")
    _, rows, columns = own.shape
    vmem = pl.BlockSpec(memory_space=pltpu.VMEM)
    parts = 4
    copies = parts * (2 * (n_scan // CORES) + 1)
    return pl.pallas_call(
        functools.partial(rim_kernel, n_tile, n_scan, wave, parts),
        out_shape=jax.ShapeDtypeStruct((2, rows + wave, columns), jnp.float32),
        in_specs=[pl.BlockSpec(memory_space=pltpu.HBM)],
        out_specs=vmem,
        scratch_shapes=[
            pltpu.SemaphoreType.DMA((copies,)),
            pltpu.SemaphoreType.DMA((copies,)),
            pltpu.SemaphoreType.DMA,
        ],
        compiler_params=pltpu.CompilerParams(
            collective_id=0, has_side_effects=True, vmem_limit_bytes=24 * 1024 * 1024
        ),
        name="first_rim",
    )(own)


def merge(grad, probe_grad, old, probe, scale, last, number):
    n_tile, n_scan = lax.axis_size("tile"), lax.axis_size("scan")
    chips = n_scan // CORES
    _, wave, _ = probe.shape
    _, extent, columns = grad.shape
    rows = extent - wave
    head = wave // chips
    fine = head // probe_parts_of(n_tile, chips, wave)
    vmem = pl.BlockSpec(memory_space=pltpu.VMEM)
    parts = 4
    copies = 8 + (6 + parts) * chips + 2 * n_tile + 5 * parts
    return pl.pallas_call(
        functools.partial(merge_kernel, n_tile, n_scan, parts, scale, last),
        out_shape=(
            jax.ShapeDtypeStruct((2, rows if last else extent, columns), jnp.float32),
            jax.ShapeDtypeStruct(probe.shape, jnp.float32),
        ),
        in_specs=[vmem] * 4,
        out_specs=(vmem, vmem),
        scratch_shapes=[
            pltpu.VMEM((extent, columns), jnp.float32),
            pltpu.VMEM((wave, wave), jnp.float32),
            pltpu.VMEM((extent, columns), jnp.float32),
            pltpu.VMEM((wave, wave), jnp.float32),
            pltpu.VMEM((chips, rows, columns), jnp.float32),
            pltpu.VMEM((chips, head, wave), jnp.float32),
            pltpu.VMEM((wave, columns), jnp.float32),
            pltpu.VMEM((n_tile, fine, wave), jnp.float32),
            pltpu.SemaphoreType.DMA((copies,)),
            pltpu.SemaphoreType.DMA((copies,)),
        ],
        compiler_params=pltpu.CompilerParams(
            collective_id=number, has_side_effects=True, vmem_limit_bytes=32 * 1024 * 1024
        ),
        name="merge_last" if last else "merge",
    )(grad, probe_grad, old, probe)


def body(object_field, probe_field, amplitudes, anchors, jitter, counts):
    wave = probe_field.shape[1]
    slots = amplitudes.shape[2]
    table_a, table_b = tables(wave)
    starts = (anchors + jitter)[0, 0]
    total_scans = slots * lax.axis_size("tile") * lax.axis_size("scan")
    scale = 1.0 / math.sqrt(total_scans)
    padded = first_rim(object_field, wave)
    probe = probe_field
    for iteration in range(ITERS):
        last = iteration == ITERS - 1
        grad, probe_grad = scan_terms(
            starts, counts, padded, probe, amplitudes, table_a, table_b
        )
        padded, probe = merge(grad, probe_grad, padded, probe, scale, last, 1 + iteration)
    return (padded, probe)


def solution(mesh):
    in_specs = (
        P(None, ("groups", "tile"), None),
        P(None, "groups", None),
        P(("groups", "tile"), "scan", None, None, None),
        P(("groups", "tile"), "scan", None, None),
        P(("groups", "tile"), "scan", None, None),
        P(("groups", "tile"), "scan"),
    )
    out_specs = (P(None, ("groups", "tile"), None), P(None, "groups", None))
    return jax.shard_map(body, mesh=mesh, in_specs=in_specs, out_specs=out_specs, check_vma=False)
```
